512 devices in a mesh: row: 16 (over y, x_hi), col: 2 (over core), depth: 16 (over z, x_lo).
Axes of the slice: x: 4 (x_hi: 2, x_lo: 2; x = x_hi * 2 + x_lo), y: 8, z: 8, core: 2. Of those that a mesh axis runs over, the one named last changes fastest.
Arguments:
- y_blocks: float32 [4096, 4096], P('row', 'col'), may hold values from -6 to 6
- z_blocks: float32 [4096, 4096], P('row', 'col'), may hold values from -0.125 to 0.125
- h_blocks: float32 [4096, 4096], P('row', 'col'), may hold values from -0.125 to 0.125
- s_pattern: int32 [16, 16], replicated, may hold values 0 or 1
- h_pattern: int32 [16, 16], replicated, may hold values 0 or 1
- keep_mask: int32 [16, 16], replicated, may hold values 0 or 1
Outputs:
- z_next: float32 [4096, 4096], P('row', 'col')
- h_times_z: float32 [4096, 4096], P('row', 'col')
The draws below stay inside these ranges and needn't reach their ends.
All inputs are finite; a program needn't handle non-finite values.
Results may differ from the reference program's by a relative error of at most 0.00013.
Values sent between devices are 32-bit elements; how exact they have to be, the bound alone decides.
No kernel may reach another device: no remote copies, remote signals or barrier semaphores. Data moves between devices by JAX's collectives and lax.ppermute only.
A program may use at most 128 MiB of HBM per device.

```python
import jax
import jax.numpy as jnp
from jax import lax

BLK = 256
NBLK = 16
ORDER = 4096


def plant(values, own_key, low, top_value):
    shape = values.shape
    index_at = [jax.random.randint(jax.random.fold_in(own_key, axis), (), 0, shape[axis]) for axis in range(len(shape))]
    values = values.at[tuple(index_at)].set(low)
    longest = shape.index(max(shape))
    index_at[longest] = (index_at[longest] + 1) % shape[longest]
    return values.at[tuple(index_at)].set(top_value)


def block_scale(key, dims, split, low, high):
    level = 1.0
    for position, blocks in split:
        steps = jax.random.uniform(jax.random.fold_in(jax.random.fold_in(key, 6), position), (blocks,), jnp.float32, low / len(split), high / len(split))
        level = level * jnp.repeat(jnp.exp(steps), dims[position] // blocks).reshape((-1,) + (1,) * (len(dims) - 1 - position))
    return level


def scatter_about(own_key, dims, scale, reach, split=(), kind=jnp.bfloat16):
    array = scale * jax.random.normal(own_key, dims, jnp.float32)
    if split:
        array = array * block_scale(own_key, dims, split, -0.22, 0.18)
    return jnp.clip(array, -reach, reach).astype(kind)


def setup_inputs(seed: int = 0) -> dict:
    splits = jax.random.split(jax.random.key(seed), 7)
    y_blocks = scatter_about(splits[0], (ORDER, ORDER), 1.0, 6.0, ((0, 16), (1, 2)), jnp.float32)
    z_blocks = scatter_about(splits[1], (ORDER, ORDER), (ORDER // 2) ** -0.5, 0.125, ((0, 16), (1, 2)), jnp.float32)
    h_blocks = scatter_about(splits[2], (ORDER, ORDER), (ORDER // 2) ** -0.5, 0.125, ((0, 16), (1, 2)), jnp.float32)
    s_pattern = plant((jax.random.randint(splits[3], (NBLK, NBLK), 0, 2) < 1).astype(jnp.int32), jax.random.fold_in(splits[3], 1), 0, 1)
    h_pattern = plant((jax.random.randint(splits[4], (NBLK, NBLK), 0, 2) < 1).astype(jnp.int32), jax.random.fold_in(splits[4], 1), 0, 1)
    keep_mask = plant((jax.random.randint(splits[5], (NBLK, NBLK), 0, 2) < 1).astype(jnp.int32), jax.random.fold_in(splits[5], 1), 0, 1)
    return dict(y_blocks=y_blocks, z_blocks=z_blocks, h_blocks=h_blocks, s_pattern=s_pattern, h_pattern=h_pattern, keep_mask=keep_mask)


def expand(pattern):
    values = pattern.astype(jnp.float32)
    return jnp.repeat(jnp.repeat(values, BLK, axis=0), BLK, axis=1)


def product(left, right):
    return jnp.dot(left, right, preferred_element_type=jnp.float32, precision=lax.Precision.HIGHEST)


def reference(y_blocks, z_blocks, h_blocks, s_pattern, h_pattern, keep_mask):
    s_full = expand(s_pattern)
    keep_full = expand(keep_mask)
    masked_y = y_blocks * s_full
    masked_z = z_blocks * s_full
    masked_h = h_blocks * expand(h_pattern)
    t_matrix = keep_full * product(masked_z, masked_y)
    identity = jnp.eye(ORDER, dtype=jnp.float32)
    q_matrix = 1.5 * identity - 0.5 * t_matrix
    z_next = keep_full * product(q_matrix, masked_z)
    h_times_z = keep_full * product(masked_h, z_next)
    return (z_next, h_times_z)
```

```python
import jax
import jax.numpy as jnp
from jax import lax
from jax.sharding import Mesh
from jax.sharding import PartitionSpec as P

X = ("xh", "xl")
ROW = ("y", "xh")
DEPTH = ("z", "xl")
HIGH = lax.Precision.HIGH


def spread(piece, axis, n):
    copies = jnp.broadcast_to(piece[None], (n,) + piece.shape)
    return lax.all_to_all(copies, axis, split_axis=0, concat_axis=0, tiled=True)


def swap_core(array):
    return lax.ppermute(array, "core", [(0, 1), (1, 0)])


def local(y_blocks, z_blocks, h_blocks, s_pattern, h_pattern, keep_mask):
    blk, width = y_blocks.shape
    half = blk // 2
    per_core = width // blk
    ny, nz = lax.axis_size("y"), lax.axis_size("z")
    y = lax.axis_index("y")
    xh = lax.axis_index("xh")
    core = lax.axis_index("core")
    z = lax.axis_index("z")
    xl = lax.axis_index("xl")
    row = 2 * y + xh
    panel = z ^ core
    column = per_core * core + panel
    keep = keep_mask.astype(jnp.float32)
    fill = s_pattern.astype(jnp.float32)

    def masked(values, pattern):
        mine = lax.dynamic_slice(pattern.astype(jnp.float32), (row, per_core * core), (1, per_core))
        return values * jnp.repeat(mine, blk, axis=1)

    def left(values):
        parts = values.reshape(blk, per_core // 2, 2, 2, half)

        def pick(a, b):
            part = lax.dynamic_slice(
                parts, (0, 0, a, b, 0), (blk, per_core // 2, 1, 1, half)
            )
            return part.reshape(blk, width // 4)

        own = pick(xh, xl)
        other = lax.ppermute(pick(1 - xh, 1 - xl), X, [(0, 3), (3, 0), (1, 2), (2, 1)])
        upper = jnp.where(xh == 0, own, other)
        lower = jnp.where(xh == 0, other, own)
        mine = jnp.concatenate([upper, lower], axis=0)
        return mine, swap_core(mine)

    def multiply(a, b):
        mine, theirs = a
        inner = mine.shape[1]
        b_mine = lax.dynamic_slice_in_dim(b, core * inner, inner, 0)
        b_theirs = lax.dynamic_slice_in_dim(b, (1 - core) * inner, inner, 0)
        return jnp.dot(mine, b_mine, precision=HIGH) + jnp.dot(theirs, b_theirs, precision=HIGH)

    def piece(values):
        return lax.dynamic_slice(values, (xl * half, panel * blk), (half, blk))

    def sum_x(parts):
        return jnp.sum(lax.all_to_all(parts, X, split_axis=0, concat_axis=0, tiled=True), axis=0)

    def finish(partial):
        return sum_x(partial.reshape(4, half, blk)) * keep[row, column]

    def gathered(all_parts):
        parts = all_parts.reshape(nz // 2, 2, 2, half, blk)
        parts = jnp.where(core == 0, parts, parts[:, ::-1])
        return parts.transpose(2, 3, 0, 1, 4).reshape(blk, width)

    masked_z = masked(z_blocks, fill)
    y_panel = spread(piece(y_blocks) * fill[row, column], "y", ny).reshape(ny * half, blk)
    z_left = left(masked_z)
    z_panel = lax.all_gather(piece(masked_z), "y", axis=0)
    t_part = multiply(z_left, y_panel)
    mine = lax.dynamic_slice_in_dim(t_part, core * blk, blk, 0)
    theirs = swap_core(lax.dynamic_slice_in_dim(t_part, (1 - core) * blk, blk, 0))
    even = (panel % 2) == 0
    blocks = jnp.stack([jnp.where(even, mine, theirs), jnp.where(even, theirs, mine)])
    blocks = blocks.reshape(2, blk, 2, half).transpose(0, 2, 1, 3).reshape(4, blk, half)
    t_share = sum_x(blocks)
    t_row = 2 * y + core
    source = (z ^ xh) & 1
    t_col = per_core * source + (z ^ source)
    at_row = t_row * blk + lax.broadcasted_iota(jnp.int32, (blk, half), 0)
    at_col = t_col * blk + xl * half + lax.broadcasted_iota(jnp.int32, (blk, half), 1)
    q_share = jnp.where(at_row == at_col, 1.5, 0.0) - 0.5 * (keep[t_row, t_col] * t_share)
    q_mine = spread(q_share, "z", nz)
    q_theirs = swap_core(q_mine)
    ordered = z_panel.reshape(2, ny // 2, half, blk).transpose(1, 0, 2, 3)
    ordered = jnp.where(xh == 0, ordered, ordered[:, ::-1]).reshape(ny * half, blk)

    def rows_of(q):
        q = q.transpose(1, 0, 2).reshape(blk, nz * half)
        return jnp.dot(q, ordered, precision=HIGH)

    z_mine, z_theirs = rows_of(q_mine), rows_of(q_theirs)
    first = core == 0
    z_share = finish(
        jnp.stack([jnp.where(first, z_mine, z_theirs), jnp.where(first, z_theirs, z_mine)])
    )
    z_next_panel = spread(z_share, "y", ny).reshape(ny * half, blk)
    z_next = gathered(lax.all_gather(z_share, DEPTH, axis=0))
    h_left = left(masked(h_blocks, h_pattern))
    h_share = finish(multiply(h_left, z_next_panel))
    h_times_z = gathered(spread(h_share, DEPTH, 2 * nz))
    return (z_next, h_times_z)


def solution(mesh):
    parts = Mesh(mesh.devices.reshape(8, 2, 2, 8, 2), ("y", "xh", "core", "z", "xl"))
    spec = P(ROW, "core")
    return jax.shard_map(
        local,
        mesh=parts,
        in_specs=(spec, spec, spec, P(), P(), P()),
        out_specs=(spec, spec),
        check_vma=False,
    )
```

```python
import jax
import jax.numpy as jnp
from jax import lax
from jax.experimental import pallas as pl
from jax.experimental.pallas import tpu as pltpu
from jax.sharding import Mesh
from jax.sharding import PartitionSpec as P

X = ("xh", "xl")
ROW = ("y", "xh")
HIGH = lax.Precision.HIGH


def spread(piece, axis, n):
    copies = jnp.broadcast_to(piece[None], (n,) + piece.shape)
    return lax.all_to_all(copies, axis, split_axis=0, concat_axis=0, tiled=True)


def swap(array, axis):
    return lax.ppermute(array, axis, [(0, 1), (1, 0)])


def place(own, other, blk):
    layers = own[0].shape[0]
    rows = own[0].shape[1]
    n = len(own)

    def kernel(*refs):
        out, sem = refs[2 * n], refs[2 * n + 1]
        xl = lax.axis_index("xl")
        core = lax.axis_index("core")
        copies = []
        for k in range(2 * n):
            mine = xl if k < n else 1 - xl
            at = pl.multiple_of(mine * (n * rows) + (k % n) * rows, rows)
            for layer in range(layers):
                to = pl.multiple_of((layer ^ core) * blk, blk)
                copies.append(
                    pltpu.make_async_copy(
                        refs[k].at[layer],
                        out.at[pl.ds(at, rows), pl.ds(to, blk)],
                        sem.at[k * layers + layer],
                    )
                )
        for copy in copies:
            copy.start()
        for copy in copies:
            copy.wait()

    return pl.pallas_call(
        kernel,
        out_shape=jax.ShapeDtypeStruct((2 * n * rows, layers * blk), own[0].dtype),
        in_specs=[pl.BlockSpec(memory_space=pl.ANY)] * (2 * n),
        out_specs=pl.BlockSpec(memory_space=pl.ANY),
        scratch_shapes=[pltpu.SemaphoreType.DMA((2 * n * layers,))],
    )(*own, *other)


def local(y_blocks, z_blocks, h_blocks, s_pattern, h_pattern, keep_mask):
    blk, width = y_blocks.shape
    half = blk // 2
    per_core = width // blk
    ny, nz = lax.axis_size("y"), lax.axis_size("z")
    y = lax.axis_index("y")
    xh = lax.axis_index("xh")
    core = lax.axis_index("core")
    z = lax.axis_index("z")
    xl = lax.axis_index("xl")
    row = 2 * y + xh
    panel = z ^ core
    column = per_core * core + panel
    keep = keep_mask.astype(jnp.float32)
    fill = s_pattern.astype(jnp.float32)

    def left(values, pattern):
        def pick(a, b):
            return jnp.concatenate(
                [
                    lax.dynamic_slice(values, (0, (2 * m + a) * blk + b * half), (blk, half))
                    * pattern[row, per_core * core + 2 * m + a]
                    for m in range(per_core // 2)
                ],
                axis=1,
            )

        own = pick(xh, xl)
        other = lax.ppermute(pick(1 - xh, 1 - xl), X, [(0, 3), (3, 0), (1, 2), (2, 1)])
        return own, other

    def multiply(mine, theirs, b):
        inner = mine.shape[1]
        b_mine = lax.dynamic_slice_in_dim(b, core * inner, inner, 0)
        b_theirs = lax.dynamic_slice_in_dim(b, (1 - core) * inner, inner, 0)
        return jnp.dot(mine, b_mine, precision=HIGH) + jnp.dot(theirs, b_theirs, precision=HIGH)

    def piece(values):
        return lax.dynamic_slice(values, (xl * half, panel * blk), (half, blk)) * fill[row, column]

    def sum_x(parts):
        return jnp.sum(lax.all_to_all(parts, X, split_axis=0, concat_axis=0, tiled=True), axis=0)

    def finish(partial):
        return sum_x(partial.reshape(4, half, blk)) * keep[row, column]

    y_copies = jnp.broadcast_to(piece(y_blocks)[None], (ny, half, blk))
    y_copies, z_blocks, h_blocks = lax.optimization_barrier((y_copies, z_blocks, h_blocks))
    y_panel = lax.all_to_all(y_copies, "y", split_axis=0, concat_axis=0, tiled=True)
    y_panel = y_panel.reshape(ny * half, blk)
    z_panel = lax.all_gather(piece(z_blocks), "y", axis=0)
    z_left = jnp.concatenate(left(z_blocks, fill), axis=0)
    t_part = multiply(z_left, swap(z_left, "core"), y_panel)
    at = (core ^ xh) * blk
    mine = lax.dynamic_slice_in_dim(t_part, at, blk, 0)
    theirs = swap(lax.dynamic_slice_in_dim(t_part, blk - at, blk, 0), "core")
    even = (panel % 2) == 0
    blocks = jnp.stack([jnp.where(even, mine, theirs), jnp.where(even, theirs, mine)])
    blocks = blocks.reshape(2, blk, 2, half).transpose(0, 2, 1, 3).reshape(4, blk, half)
    blocks, z_panel = lax.optimization_barrier((blocks, z_panel))
    t_share = sum_x(blocks)
    t_row = 2 * y + core
    source = (z ^ xh) & 1
    t_col = per_core * source + (z ^ source)
    at_row = t_row * blk + lax.broadcasted_iota(jnp.int32, (blk, half), 0)
    at_col = t_col * blk + xl * half + lax.broadcasted_iota(jnp.int32, (blk, half), 1)
    q_share = jnp.where(at_row == at_col, 1.5, 0.0) - 0.5 * (keep[t_row, t_col] * t_share)
    q_mine = spread(q_share, "z", nz)
    q_theirs = swap(q_mine, "core")
    ordered = z_panel.reshape(2, ny // 2, half, blk).transpose(1, 0, 2, 3)
    ordered = jnp.where(xh == 0, ordered, ordered[:, ::-1]).reshape(ny * half, blk)

    def rows_of(q):
        q = q.transpose(1, 0, 2).reshape(blk, nz * half)
        return jnp.dot(q, ordered, precision=HIGH)

    z_mine, z_theirs = rows_of(q_mine), rows_of(q_theirs)
    first = core == 0
    z_share = finish(
        jnp.stack([jnp.where(first, z_mine, z_theirs), jnp.where(first, z_theirs, z_mine)])
    )
    z_next_panel = spread(z_share, "y", ny).reshape(ny * half, blk)
    z_own = lax.all_gather(z_share, "z", axis=0)
    own, other = left(h_blocks, h_pattern.astype(jnp.float32))
    own, other = jnp.where(xh == 0, own, other), jnp.where(xh == 0, other, own)
    h_left = jnp.concatenate([own, other], axis=0)
    h_partial = multiply(h_left, swap(h_left, "core"), z_next_panel)
    h_share = finish(h_partial)
    h_share, z_own = lax.optimization_barrier((h_share, z_own))
    z_next = place([z_own], [swap(z_own, "xl")], blk)
    h_own = [spread(h_share[k * half // 2 : (k + 1) * half // 2], "z", nz) for k in range(2)]
    h_times_z = place(h_own, [swap(part, "xl") for part in h_own], blk)
    return (z_next, h_times_z)


def solution(mesh):
    parts = Mesh(mesh.devices.reshape(8, 2, 2, 8, 2), ("y", "xh", "core", "z", "xl"))
    spec = P(ROW, "core")
    return jax.shard_map(
        local,
        mesh=parts,
        in_specs=(spec, spec, spec, P(), P(), P()),
        out_specs=(spec, spec),
        check_vma=False,
    )
```

```python
import jax
import jax.numpy as jnp
from jax import lax
from jax.experimental import pallas as pl
from jax.experimental.pallas import tpu as pltpu
from jax.sharding import Mesh
from jax.sharding import PartitionSpec as P

X = ("xh", "xl")
ROW = ("y", "xh")
HIGH = lax.Precision.HIGH


def spread(piece, axis, n):
    copies = jnp.broadcast_to(piece[None], (n,) + piece.shape)
    return lax.all_to_all(copies, axis, split_axis=0, concat_axis=0, tiled=True)


def swap(array, axis):
    return lax.ppermute(array, axis, [(0, 1), (1, 0)])


def place(own, other, blk):
    layers = own[0].shape[0]
    rows = own[0].shape[1]
    n = len(own)

    def kernel(*refs):
        out = refs[2 * n]
        xl = lax.axis_index("xl")
        core = lax.axis_index("core")
        for k in range(2 * n):
            mine = xl if k < n else 1 - xl
            at = pl.multiple_of(mine * (n * rows) + (k % n) * rows, rows)
            for layer in range(layers):
                to = pl.multiple_of((layer ^ core) * blk, blk)
                out[pl.ds(at, rows), pl.ds(to, blk)] = refs[k][layer]

    return pl.pallas_call(
        kernel,
        out_shape=jax.ShapeDtypeStruct((2 * n * rows, layers * blk), own[0].dtype),
        in_specs=[pl.BlockSpec(memory_space=pltpu.VMEM)] * (2 * n),
        out_specs=pl.BlockSpec(memory_space=pltpu.VMEM),
        compiler_params=pltpu.CompilerParams(vmem_limit_bytes=24 * 1024 * 1024),
    )(*own, *other)


def local(y_blocks, z_blocks, h_blocks, s_pattern, h_pattern, keep_mask):
    blk, width = y_blocks.shape
    half = blk // 2
    per_core = width // blk
    ny, nz = lax.axis_size("y"), lax.axis_size("z")
    y = lax.axis_index("y")
    xh = lax.axis_index("xh")
    core = lax.axis_index("core")
    z = lax.axis_index("z")
    xl = lax.axis_index("xl")
    row = 2 * y + xh
    panel = z ^ core
    column = per_core * core + panel
    keep = keep_mask.astype(jnp.float32)
    fill = s_pattern.astype(jnp.float32)

    def left(values, pattern):
        def pick(a, b):
            return jnp.concatenate(
                [
                    lax.dynamic_slice(values, (0, (2 * m + a) * blk + b * half), (blk, half))
                    * pattern[row, per_core * core + 2 * m + a]
                    for m in range(per_core // 2)
                ],
                axis=1,
            )

        own = pick(xh, xl)
        other = lax.ppermute(pick(1 - xh, 1 - xl), X, [(0, 3), (3, 0), (1, 2), (2, 1)])
        return own, other

    def multiply(mine, theirs, b):
        inner = mine.shape[1]
        b_mine = lax.dynamic_slice_in_dim(b, core * inner, inner, 0)
        b_theirs = lax.dynamic_slice_in_dim(b, (1 - core) * inner, inner, 0)
        return jnp.dot(mine, b_mine, precision=HIGH) + jnp.dot(theirs, b_theirs, precision=HIGH)

    def piece(values):
        return lax.dynamic_slice(values, (xl * half, panel * blk), (half, blk)) * fill[row, column]

    def sum_x(parts):
        return jnp.sum(lax.all_to_all(parts, X, split_axis=0, concat_axis=0, tiled=True), axis=0)

    def finish(partial):
        return sum_x(partial.reshape(4, half, blk)) * keep[row, column]

    y_copies = jnp.broadcast_to(piece(y_blocks)[None], (ny, half, blk))
    y_copies, z_blocks, h_blocks = lax.optimization_barrier((y_copies, z_blocks, h_blocks))
    y_panel = lax.all_to_all(y_copies, "y", split_axis=0, concat_axis=0, tiled=True)
    y_panel = y_panel.reshape(ny * half, blk)
    z_panel = lax.all_gather(piece(z_blocks), "y", axis=0)
    z_left = jnp.concatenate(left(z_blocks, fill), axis=0)
    t_part = multiply(z_left, swap(z_left, "core"), y_panel)
    at = (core ^ xh) * blk
    mine = lax.dynamic_slice_in_dim(t_part, at, blk, 0)
    theirs = swap(lax.dynamic_slice_in_dim(t_part, blk - at, blk, 0), "core")
    even = (panel % 2) == 0
    blocks = jnp.stack([jnp.where(even, mine, theirs), jnp.where(even, theirs, mine)])
    blocks = blocks.reshape(2, blk, 2, half).transpose(0, 2, 1, 3).reshape(4, blk, half)
    t_share = sum_x(blocks)
    t_row = 2 * y + core
    source = (z ^ xh) & 1
    t_col = per_core * source + (z ^ source)
    at_row = t_row * blk + lax.broadcasted_iota(jnp.int32, (blk, half), 0)
    at_col = t_col * blk + xl * half + lax.broadcasted_iota(jnp.int32, (blk, half), 1)
    q_share = jnp.where(at_row == at_col, 1.5, 0.0) - 0.5 * (keep[t_row, t_col] * t_share)
    q_share, z_panel = lax.optimization_barrier((q_share, z_panel))
    q_mine = spread(q_share, "z", nz)
    q_theirs = swap(q_mine, "core")
    ordered = z_panel.reshape(2, ny // 2, half, blk).transpose(1, 0, 2, 3)
    ordered = jnp.where(xh == 0, ordered, ordered[:, ::-1]).reshape(ny * half, blk)

    def rows_of(q):
        q = q.transpose(1, 0, 2).reshape(blk, nz * half)
        return jnp.dot(q, ordered, precision=HIGH)

    z_mine, z_theirs = rows_of(q_mine), rows_of(q_theirs)
    first = core == 0
    z_share = finish(
        jnp.stack([jnp.where(first, z_mine, z_theirs), jnp.where(first, z_theirs, z_mine)])
    )
    z_next_panel = spread(z_share, "y", ny).reshape(ny * half, blk)
    z_own = lax.all_gather(z_share, "z", axis=0)
    own, other = left(h_blocks, h_pattern.astype(jnp.float32))
    own, other = jnp.where(xh == 0, own, other), jnp.where(xh == 0, other, own)
    h_left = jnp.concatenate([own, other], axis=0)
    h_partial = multiply(h_left, swap(h_left, "core"), z_next_panel)
    h_share = finish(h_partial)
    h_share, z_own = lax.optimization_barrier((h_share, z_own))
    z_next = place([z_own], [swap(z_own, "xl")], blk)
    h_own = [spread(h_share[k * half // 2 : (k + 1) * half // 2], "z", nz) for k in range(2)]
    h_times_z = place(h_own, [swap(part, "xl") for part in h_own], blk)
    return (z_next, h_times_z)


def solution(mesh):
    parts = Mesh(mesh.devices.reshape(8, 2, 2, 8, 2), ("y", "xh", "core", "z", "xl"))
    spec = P(ROW, "core")
    return jax.shard_map(
        local,
        mesh=parts,
        in_specs=(spec, spec, spec, P(), P(), P()),
        out_specs=(spec, spec),
        check_vma=False,
    )
```

```python
import jax
import jax.numpy as jnp
from jax import lax
from jax.experimental import pallas as pl
from jax.experimental.pallas import tpu as pltpu
from jax.sharding import Mesh
from jax.sharding import PartitionSpec as P

X = ("xh", "xl")
ROW = ("y", "xh")
DEPTH = ("z", "xl")
PLANE = ("xh", "core", "z", "xl")
HIGH = lax.Precision.HIGH
CHUNKS = 2


def copies_of(piece, n):
    return jnp.broadcast_to(piece[None], (n,) + piece.shape)


def spread(copies, axis):
    return lax.all_to_all(copies, axis, split_axis=0, concat_axis=0, tiled=True)


def swap(array, axis):
    return lax.ppermute(array, axis, [(0, 1), (1, 0)])


def after(array, other):
    return lax.optimization_barrier((array, other))[0]


def place(parts, places, shape):
    def kernel(*refs):
        out = refs[-1]
        for part, index, row, column, rows, columns in places():
            out[pl.ds(row, rows), pl.ds(column, columns)] = refs[part][index]

    return pl.pallas_call(
        kernel,
        out_shape=jax.ShapeDtypeStruct(shape, parts[0].dtype),
        in_specs=[pl.BlockSpec(memory_space=pltpu.VMEM)] * len(parts),
        out_specs=pl.BlockSpec(memory_space=pltpu.VMEM),
        compiler_params=pltpu.CompilerParams(vmem_limit_bytes=24 * 1024 * 1024),
    )(*parts)


def local(y_blocks, z_blocks, h_blocks, s_pattern, h_pattern, keep_mask):
    blk, width = y_blocks.shape
    half, quarter = blk // 2, blk // 4
    per_core = width // blk
    ny, nz = lax.axis_size("y"), lax.axis_size("z")
    y = lax.axis_index("y")
    xh = lax.axis_index("xh")
    core = lax.axis_index("core")
    z = lax.axis_index("z")
    xl = lax.axis_index("xl")
    row = 2 * y + xh
    panel = z ^ core
    column = per_core * core + panel
    keep = keep_mask.astype(jnp.float32)
    fill = s_pattern.astype(jnp.float32)


    def left(values, pattern, wait=None):
        def pick(a, b):
            return jnp.concatenate(
                [
                    lax.dynamic_slice(values, (0, (2 * m + a) * blk + b * half), (blk, half))
                    * pattern[row, per_core * core + 2 * m + a]
                    for m in range(per_core // 2)
                ],
                axis=1,
            )

        own = pick(xh, xl)
        other = lax.ppermute(pick(1 - xh, 1 - xl), X, [(0, 3), (3, 0), (1, 2), (2, 1)])
        if wait is not None:
            other = after(other, wait)
        return jnp.concatenate([own, other], axis=0)

    def halves(array):
        inner = array.shape[0] // 2
        return [lax.dynamic_slice_in_dim(array, at * inner, inner, 0) for at in (core, 1 - core)]

    def dot(a, b, dims):
        return lax.dot_general(
            a, b, ((dims[:1], dims[1:]), ((), ())), precision=HIGH, preferred_element_type=jnp.float32
        )

    def sum_x(array, first):
        def share(a, b):
            at = (a ^ first) * blk + b * half
            return lax.dynamic_slice_in_dim(array, at, half, 0)

        total = share(xh, xl)
        for a, b in ((0, 1), (1, 1), (1, 0)):
            pairs = [(i, i ^ (2 * a + b)) for i in range(4)]
            total = total + lax.ppermute(share(xh ^ a, xl ^ b), X, pairs)
        return total * keep[row, column]

    def chunk(array, k):
        return array[:, k * half : (k + 1) * half]

    y_piece = lax.dynamic_slice(y_blocks, (xl * half, panel * blk), (half, blk)) * fill[row, column]
    y_copies = [copies_of(chunk(y_piece, k), ny) for k in range(CHUNKS)]
    y_copies[0], z_blocks, h_blocks = lax.optimization_barrier((y_copies[0], z_blocks, h_blocks))
    y_panels = [spread(y_copies[0], "y")]
    y_panels.append(spread(after(y_copies[1], y_panels[0]), "y"))
    z_piece = jnp.concatenate(
        [
            lax.dynamic_slice(z_blocks, (k * half + xl * quarter, panel * blk), (quarter, blk))
            for k in range(CHUNKS)
        ],
        axis=0,
    )
    z_panel = lax.all_gather(z_piece * fill[row, column], "y", axis=0)
    z_left = left(z_blocks, fill, y_panels[0])
    z_lefts = (z_left, swap(z_left, "core"))
    t_row = 2 * y + core
    source = (z ^ xh) & 1
    t_col = per_core * source + (z ^ source)

    def t_share(y_panel):
        partial = sum(
            dot(b, a, (0, 1)) for a, b in zip(z_lefts, halves(y_panel.reshape(ny * half, half)))
        )
        total = None
        for s in range(4):
            to_xl, to_core = xh ^ (s >> 1), xl ^ (s & 1)
            pairs = []
            for a in range(2):
                for c in range(2):
                    for zz in range(8):
                        for b in range(2):
                            to_xh = (zz ^ c) & 1
                            to = ((to_xh * 2 + (b ^ (s & 1))) * 8 + zz) * 2 + (a ^ (s >> 1))
                            pairs.append((((a * 2 + c) * 8 + zz) * 2 + b, to))
            share = lax.dynamic_slice(
                partial, (to_xl * quarter, (to_core ^ xh) * blk), (quarter, blk)
            )
            got = lax.ppermute(share, PLANE, pairs)
            total = got if total is None else total + got
        return total

    q_mine, q_theirs = [], []
    ordered = z_panel.reshape(2, ny // 2, CHUNKS, quarter, blk).transpose(2, 1, 0, 3, 4)
    ordered = jnp.where(xh == 0, ordered, ordered[:, :, ::-1]).reshape(CHUNKS, ny * quarter, blk)
    last = y_panels[1]
    for k in range(CHUNKS):
        at_col = lax.broadcasted_iota(jnp.int32, (quarter, blk), 0) + k * half + xl * quarter
        at_row = lax.broadcasted_iota(jnp.int32, (quarter, blk), 1)
        diagonal = (t_row == t_col) & (at_row == at_col)
        q_share = jnp.where(diagonal, 1.5, 0.0) - 0.5 * (keep[t_row, t_col] * t_share(y_panels[k]))
        q = spread(after(copies_of(q_share, nz), last), "z")
        last = q
        q_mine.append(q.reshape(nz * quarter, blk))
        q_theirs.append(swap(q, "core").reshape(nz * quarter, blk))
    z_both = jnp.concatenate(
        [sum(dot(q[k], ordered[k], (0, 0)) for k in range(CHUNKS)) for q in (q_mine, q_theirs)], axis=0
    )
    z_shares = [sum_x(chunk(z_both, 0), core)]
    z_copies = copies_of(z_shares[0], ny)
    z_shares.append(sum_x(chunk(after(z_both, z_copies), 1), core))
    z_all = [lax.all_gather(share, DEPTH, axis=0) for share in z_shares]
    panels = [spread(z_copies, "y")]
    panels.append(spread(after(copies_of(z_shares[1], ny), panels[0]), "y"))
    h_left = left(h_blocks, h_pattern.astype(jnp.float32))
    h_lefts = (h_left, swap(h_left, "core"))
    h_own = []
    last = panels[1]
    for k in range(CHUNKS):
        partial = sum(
            dot(a, b, (1, 0)) for a, b in zip(h_lefts, halves(panels[k].reshape(ny * half, half)))
        )
        h_own.append(spread(after(copies_of(sum_x(partial, xh), nz), last), "z"))
        last = (h_own[-1], z_all[0])
    h_other = [swap(part, "xl") for part in h_own]

    def column_of(layer, k):
        return pl.multiple_of((layer ^ lax.axis_index("core")) * blk + k * half, half)

    def z_places():
        return [
            (k, 2 * layer + b, b * half, column_of(layer, k), half, half)
            for k in range(CHUNKS)
            for layer in range(nz)
            for b in range(2)
        ]

    def h_places():
        mine = lax.axis_index("xl")
        return [
            (k + CHUNKS * b, layer, pl.multiple_of((mine ^ b) * half, half), column_of(layer, k), half, half)
            for k in range(CHUNKS)
            for layer in range(nz)
            for b in range(2)
        ]

    return (
        place(z_all, z_places, (blk, width)),
        place(h_own + h_other, h_places, (blk, width)),
    )


def solution(mesh):
    parts = Mesh(mesh.devices.reshape(8, 2, 2, 8, 2), ("y", "xh", "core", "z", "xl"))
    spec = P(ROW, "core")
    return jax.shard_map(
        local,
        mesh=parts,
        in_specs=(spec, spec, spec, P(), P(), P()),
        out_specs=(spec, spec),
        check_vma=False,
    )
```

```python
import jax
import jax.numpy as jnp
from jax import lax
from jax.experimental import pallas as pl
from jax.experimental.pallas import tpu as pltpu
from jax.sharding import Mesh
from jax.sharding import PartitionSpec as P

X = ("xh", "xl")
ROW = ("y", "xh")
HIGH = lax.Precision.HIGH


def spread(piece, axis, n):
    copies = jnp.broadcast_to(piece[None], (n,) + piece.shape)
    return lax.all_to_all(copies, axis, split_axis=0, concat_axis=0, tiled=True)


def swap(array, axis):
    return lax.ppermute(array, axis, [(0, 1), (1, 0)])


def place(parts, blk):
    layers = parts[0].shape[0]
    half = blk // 2

    def kernel(*refs):
        out = refs[-1]
        xl = lax.axis_index("xl")
        core = lax.axis_index("core")
        for share in range(2):
            at = pl.multiple_of((xl ^ share) * half, half)
            for layer in range(layers):
                to = pl.multiple_of((layer ^ core) * blk, blk)
                out[pl.ds(at, half), pl.ds(to, blk)] = refs[share][layer]

    return pl.pallas_call(
        kernel,
        out_shape=jax.ShapeDtypeStruct((blk, layers * blk), parts[0].dtype),
        in_specs=[pl.BlockSpec(memory_space=pltpu.VMEM)] * len(parts),
        out_specs=pl.BlockSpec(memory_space=pltpu.VMEM),
        compiler_params=pltpu.CompilerParams(vmem_limit_bytes=24 * 1024 * 1024),
    )(*parts)


def local(y_blocks, z_blocks, h_blocks, s_pattern, h_pattern, keep_mask):
    blk, width = y_blocks.shape
    half = blk // 2
    per_core = width // blk
    ny, nz = lax.axis_size("y"), lax.axis_size("z")
    y = lax.axis_index("y")
    xh = lax.axis_index("xh")
    core = lax.axis_index("core")
    z = lax.axis_index("z")
    xl = lax.axis_index("xl")
    row = 2 * y + xh
    panel = z ^ core
    column = per_core * core + panel
    keep = keep_mask.astype(jnp.float32)
    fill = s_pattern.astype(jnp.float32)

    def left(values, pattern):
        def pick(a, b):
            return jnp.concatenate(
                [
                    lax.dynamic_slice(values, (0, (2 * m + a) * blk + b * half), (blk, half))
                    * pattern[row, per_core * core + 2 * m + a]
                    for m in range(per_core // 2)
                ],
                axis=1,
            )

        own = pick(xh, xl)
        other = lax.ppermute(pick(1 - xh, 1 - xl), X, [(0, 3), (3, 0), (1, 2), (2, 1)])
        return own, other

    def multiply(mine, theirs, b):
        inner = mine.shape[1]
        b_mine = lax.dynamic_slice_in_dim(b, core * inner, inner, 0)
        b_theirs = lax.dynamic_slice_in_dim(b, (1 - core) * inner, inner, 0)
        return jnp.dot(mine, b_mine, precision=HIGH) + jnp.dot(theirs, b_theirs, precision=HIGH)

    def piece(values):
        return lax.dynamic_slice(values, (xl * half, panel * blk), (half, blk)) * fill[row, column]

    def sum_x(parts):
        return jnp.sum(lax.all_to_all(parts, X, split_axis=0, concat_axis=0, tiled=True), axis=0)

    def finish(partial):
        return sum_x(partial.reshape(4, half, blk)) * keep[row, column]

    y_copies = jnp.broadcast_to(piece(y_blocks)[None], (ny, half, blk))
    y_copies, z_blocks = lax.optimization_barrier((y_copies, z_blocks))
    y_panel = lax.all_to_all(y_copies, "y", split_axis=0, concat_axis=0, tiled=True)
    y_panel = y_panel.reshape(ny * half, blk)
    z_left = jnp.concatenate(left(z_blocks, fill), axis=0)
    t_part = multiply(z_left, swap(z_left, "core"), y_panel)
    at = (core ^ xh) * blk
    mine = lax.dynamic_slice_in_dim(t_part, at, blk, 0)
    theirs = swap(lax.dynamic_slice_in_dim(t_part, blk - at, blk, 0), "core")
    even = (panel % 2) == 0
    blocks = jnp.stack([jnp.where(even, mine, theirs), jnp.where(even, theirs, mine)])
    blocks = blocks.reshape(2, blk, 2, half).transpose(0, 2, 1, 3).reshape(4, blk, half)
    t_share = sum_x(blocks)
    t_row = 2 * y + core
    source = (z ^ xh) & 1
    t_col = per_core * source + (z ^ source)
    at_row = t_row * blk + lax.broadcasted_iota(jnp.int32, (blk, half), 0)
    at_col = t_col * blk + xl * half + lax.broadcasted_iota(jnp.int32, (blk, half), 1)
    q_share = jnp.where(at_row == at_col, 1.5, 0.0) - 0.5 * (keep[t_row, t_col] * t_share)
    q_mine = lax.all_gather(q_share, "z", axis=0)
    z_piece, h_blocks, _ = lax.optimization_barrier((piece(z_blocks), h_blocks, q_share))
    z_panel = spread(z_piece, "y", ny)
    q_theirs = swap(q_mine, "core")
    ordered = z_panel.reshape(2, ny // 2, half, blk).transpose(1, 0, 2, 3)
    ordered = jnp.where(xh == 0, ordered, ordered[:, ::-1]).reshape(ny * half, blk)

    def rows_of(q):
        q = q.transpose(1, 0, 2).reshape(blk, nz * half)
        return jnp.dot(q, ordered, precision=HIGH)

    own, other = left(h_blocks, h_pattern.astype(jnp.float32))
    own, other = jnp.where(xh == 0, own, other), jnp.where(xh == 0, other, own)
    h_left = jnp.concatenate([own, other], axis=0)
    h_theirs = swap(h_left, "core")
    z_mine, z_theirs = rows_of(q_mine), rows_of(q_theirs)
    z_mine, h_left, h_theirs = lax.optimization_barrier((z_mine, h_left, h_theirs))
    first = core == 0
    z_share = finish(
        jnp.stack([jnp.where(first, z_mine, z_theirs), jnp.where(first, z_theirs, z_mine)])
    )
    z_copies = jnp.broadcast_to(z_share[None], (ny, half, blk))
    z_next_panel = lax.all_to_all(z_copies, "y", split_axis=0, concat_axis=0, tiled=True)
    z_next_panel = z_next_panel.reshape(ny * half, blk)
    z_own = lax.all_gather(z_share, "z", axis=0)
    h_partial = multiply(h_left, h_theirs, z_next_panel)
    h_share = finish(h_partial)
    h_share, z_own = lax.optimization_barrier((h_share, z_own))
    h_own = lax.all_gather(h_share, "z", axis=0)
    h_swapped = swap(h_share, "xl")
    h_copies, z_own = lax.optimization_barrier(
        (jnp.broadcast_to(h_swapped[None], (nz, half, blk)), z_own)
    )
    h_other = lax.all_to_all(h_copies, "z", split_axis=0, concat_axis=0, tiled=True)
    z_next = place([z_own, swap(z_own, "xl")], blk)
    h_times_z = place([h_own, h_other], blk)
    return (z_next, h_times_z)


def solution(mesh):
    parts = Mesh(mesh.devices.reshape(8, 2, 2, 8, 2), ("y", "xh", "core", "z", "xl"))
    spec = P(ROW, "core")
    return jax.shard_map(
        local,
        mesh=parts,
        in_specs=(spec, spec, spec, P(), P(), P()),
        out_specs=(spec, spec),
        check_vma=False,
    )
```

```python
import jax
import jax.numpy as jnp
from jax import lax
from jax.experimental import pallas as pl
from jax.experimental.pallas import tpu as pltpu
from jax.sharding import Mesh
from jax.sharding import PartitionSpec as P

X = ("xh", "xl")
ROW = ("y", "xh")
HIGH = lax.Precision.HIGH


def spread(piece, axis, n):
    copies = jnp.broadcast_to(piece[None], (n,) + piece.shape)
    return lax.all_to_all(copies, axis, split_axis=0, concat_axis=0, tiled=True)


def swap(array, axis):
    return lax.ppermute(array, axis, [(0, 1), (1, 0)])


def place(parts, pieces, blk):
    layers = parts[0].shape[0]
    half = blk // 2

    def kernel(*refs):
        out = refs[-1]
        xl = lax.axis_index("xl")
        core = lax.axis_index("core")
        for part, first, share, offset, rows in pieces:
            at = pl.multiple_of((xl ^ share) * half + offset, 8)
            for layer in range(layers):
                to = pl.multiple_of((layer ^ core) * blk, blk)
                out[pl.ds(at, rows), pl.ds(to, blk)] = refs[part][layer, first : first + rows]

    return pl.pallas_call(
        kernel,
        out_shape=jax.ShapeDtypeStruct((blk, layers * blk), parts[0].dtype),
        in_specs=[pl.BlockSpec(memory_space=pltpu.VMEM)] * len(parts),
        out_specs=pl.BlockSpec(memory_space=pltpu.VMEM),
        compiler_params=pltpu.CompilerParams(vmem_limit_bytes=24 * 1024 * 1024),
    )(*parts)


def local(y_blocks, z_blocks, h_blocks, s_pattern, h_pattern, keep_mask):
    blk, width = y_blocks.shape
    half = blk // 2
    per_core = width // blk
    ny, nz = lax.axis_size("y"), lax.axis_size("z")
    y = lax.axis_index("y")
    xh = lax.axis_index("xh")
    core = lax.axis_index("core")
    z = lax.axis_index("z")
    xl = lax.axis_index("xl")
    row = 2 * y + xh
    panel = z ^ core
    column = per_core * core + panel
    keep = keep_mask.astype(jnp.float32)
    fill = s_pattern.astype(jnp.float32)

    def left(values, pattern):
        def pick(a, b):
            return jnp.concatenate(
                [
                    lax.dynamic_slice(values, (0, (2 * m + a) * blk + b * half), (blk, half))
                    * pattern[row, per_core * core + 2 * m + a]
                    for m in range(per_core // 2)
                ],
                axis=1,
            )

        own = pick(xh, xl)
        other = lax.ppermute(pick(1 - xh, 1 - xl), X, [(0, 3), (3, 0), (1, 2), (2, 1)])
        return own, other

    def multiply(mine, theirs, b):
        inner = mine.shape[1]
        b_mine = lax.dynamic_slice_in_dim(b, core * inner, inner, 0)
        b_theirs = lax.dynamic_slice_in_dim(b, (1 - core) * inner, inner, 0)
        return jnp.dot(mine, b_mine, precision=HIGH) + jnp.dot(theirs, b_theirs, precision=HIGH)

    def piece(values):
        return lax.dynamic_slice(values, (xl * half, panel * blk), (half, blk)) * fill[row, column]

    def sum_x(parts):
        return jnp.sum(lax.all_to_all(parts, X, split_axis=0, concat_axis=0, tiled=True), axis=0)

    def finish(partial):
        return sum_x(partial.reshape(4, half, blk)) * keep[row, column]

    y_copies = jnp.broadcast_to(piece(y_blocks)[None], (ny, half, blk))
    z_piece = piece(z_blocks)
    y_copies, z_piece, z_blocks = lax.optimization_barrier((y_copies, z_piece, z_blocks))
    y_panel = lax.all_to_all(y_copies, "y", split_axis=0, concat_axis=0, tiled=True)
    y_panel = y_panel.reshape(ny * half, blk)
    z_left = jnp.concatenate(left(z_blocks, fill), axis=0)
    t_part = multiply(z_left, swap(z_left, "core"), y_panel)
    at = (core ^ xh) * blk
    mine = lax.dynamic_slice_in_dim(t_part, at, blk, 0)
    theirs = swap(lax.dynamic_slice_in_dim(t_part, blk - at, blk, 0), "core")
    even = (panel % 2) == 0
    blocks = jnp.stack([jnp.where(even, mine, theirs), jnp.where(even, theirs, mine)])
    blocks = blocks.reshape(2, blk, 2, half).transpose(0, 2, 1, 3).reshape(4, blk, half)
    t_share = sum_x(blocks)
    t_row = 2 * y + core
    source = (z ^ xh) & 1
    t_col = per_core * source + (z ^ source)
    at_row = t_row * blk + lax.broadcasted_iota(jnp.int32, (blk, half), 0)
    at_col = t_col * blk + xl * half + lax.broadcasted_iota(jnp.int32, (blk, half), 1)
    q_share = jnp.where(at_row == at_col, 1.5, 0.0) - 0.5 * (keep[t_row, t_col] * t_share)
    z_panel = lax.all_gather(z_piece, "y", axis=0)
    q_share, h_blocks = lax.optimization_barrier((q_share, h_blocks))
    q_mine = spread(q_share, "z", nz)
    q_mine, z_panel = lax.optimization_barrier((q_mine, z_panel))
    q_theirs = swap(q_mine, "core")
    ordered = z_panel.reshape(2, ny // 2, half, blk).transpose(1, 0, 2, 3)
    ordered = jnp.where(xh == 0, ordered, ordered[:, ::-1]).reshape(ny * half, blk)

    def rows_of(q):
        q = q.transpose(1, 0, 2).reshape(blk, nz * half)
        return jnp.dot(q, ordered, precision=HIGH)

    own, other = left(h_blocks, h_pattern.astype(jnp.float32))
    own, other = jnp.where(xh == 0, own, other), jnp.where(xh == 0, other, own)
    h_left = jnp.concatenate([own, other], axis=0)
    h_theirs = swap(h_left, "core")
    z_mine, z_theirs = rows_of(q_mine), rows_of(q_theirs)
    z_mine, h_left, h_theirs = lax.optimization_barrier((z_mine, h_left, h_theirs))
    first = core == 0
    z_share = finish(
        jnp.stack([jnp.where(first, z_mine, z_theirs), jnp.where(first, z_theirs, z_mine)])
    )
    z_copies = jnp.broadcast_to(z_share[None], (ny, half, blk))
    z_next_panel = lax.all_to_all(z_copies, "y", split_axis=0, concat_axis=0, tiled=True)
    z_next_panel = z_next_panel.reshape(ny * half, blk)
    z_shares = jnp.concatenate([z_share, swap(z_share, "xl")], axis=0)
    z_all = lax.all_gather(z_shares, "z", axis=0)
    h_partial = multiply(h_left, h_theirs, z_next_panel)
    h_share = finish(h_partial)
    passed = half * 5 // 8
    rest = half - passed
    early = jnp.broadcast_to(h_share[:passed][None], (nz, passed, blk))
    early, h_share = lax.optimization_barrier((early, h_share))
    h_early = lax.all_to_all(early, "z", split_axis=0, concat_axis=0, tiled=True)
    late = jnp.concatenate([h_share[passed:], swap(h_share[passed:], "xl")], axis=0)
    late = jnp.broadcast_to(late[None], (nz, 2 * rest, blk))
    late, z_all, h_early = lax.optimization_barrier((late, z_all, h_early))
    h_late = lax.all_to_all(late, "z", split_axis=0, concat_axis=0, tiled=True)
    z_next = place([z_all], [(0, 0, 0, 0, half), (0, half, 1, 0, half)], blk)
    h_times_z = place(
        [h_early, h_late, swap(h_early, "xl")],
        [
            (0, 0, 0, 0, passed),
            (1, 0, 0, passed, rest),
            (1, rest, 1, passed, rest),
            (2, 0, 1, 0, passed),
        ],
        blk,
    )
    return (z_next, h_times_z)


def solution(mesh):
    parts = Mesh(mesh.devices.reshape(8, 2, 2, 8, 2), ("y", "xh", "core", "z", "xl"))
    spec = P(ROW, "core")
    return jax.shard_map(
        local,
        mesh=parts,
        in_specs=(spec, spec, spec, P(), P(), P()),
        out_specs=(spec, spec),
        check_vma=False,
    )
```

```python
import jax
import jax.numpy as jnp
from jax import lax
from jax.experimental import pallas as pl
from jax.experimental.pallas import tpu as pltpu
from jax.sharding import Mesh
from jax.sharding import PartitionSpec as P

X = ("xh", "xl")
ROW = ("y", "xh")
HIGH = lax.Precision.HIGH


def spread(piece, axis, n):
    copies = jnp.broadcast_to(piece[None], (n,) + piece.shape)
    return lax.all_to_all(copies, axis, split_axis=0, concat_axis=0, tiled=True)


def swap(array, axis):
    return lax.ppermute(array, axis, [(0, 1), (1, 0)])


def place(parts, pieces, blk):
    layers = parts[0].shape[0]
    half = blk // 2

    def kernel(*refs):
        out = refs[-1]
        xl = lax.axis_index("xl")
        core = lax.axis_index("core")
        for part, first, share, offset, rows in pieces:
            at = pl.multiple_of((xl ^ share) * half + offset, 8)
            for layer in range(layers):
                to = pl.multiple_of((layer ^ core) * blk, blk)
                out[pl.ds(at, rows), pl.ds(to, blk)] = refs[part][layer, first : first + rows]

    return pl.pallas_call(
        kernel,
        out_shape=jax.ShapeDtypeStruct((blk, layers * blk), parts[0].dtype),
        in_specs=[pl.BlockSpec(memory_space=pltpu.VMEM)] * len(parts),
        out_specs=pl.BlockSpec(memory_space=pltpu.VMEM),
        compiler_params=pltpu.CompilerParams(vmem_limit_bytes=24 * 1024 * 1024),
    )(*parts)


def local(y_blocks, z_blocks, h_blocks, s_pattern, h_pattern, keep_mask):
    blk, width = y_blocks.shape
    half = blk // 2
    per_core = width // blk
    ny, nz = lax.axis_size("y"), lax.axis_size("z")
    y = lax.axis_index("y")
    xh = lax.axis_index("xh")
    core = lax.axis_index("core")
    z = lax.axis_index("z")
    xl = lax.axis_index("xl")
    row = 2 * y + xh
    panel = z ^ core
    column = per_core * core + panel
    keep = keep_mask.astype(jnp.float32)
    fill = s_pattern.astype(jnp.float32)

    def slices(values, pattern):
        def pick(a, b):
            return jnp.concatenate(
                [
                    lax.dynamic_slice(values, (0, (2 * m + a) * blk + b * half), (blk, half))
                    * pattern[row, per_core * core + 2 * m + a]
                    for m in range(per_core // 2)
                ],
                axis=1,
            )

        part = pick(1 - xh, 1 - xl)
        part, values = lax.optimization_barrier((part, values))
        return part, pick(xh, xl)

    def rows_with_partner(part, own):
        other = lax.ppermute(part, X, [(0, 3), (3, 0), (1, 2), (2, 1)])
        return [(rows, swap(rows, "core")) for rows in (own, other)]

    def multiply(mine, theirs, b):
        inner = mine.shape[1]
        b_mine = lax.dynamic_slice_in_dim(b, core * inner, inner, 0)
        b_theirs = lax.dynamic_slice_in_dim(b, (1 - core) * inner, inner, 0)
        return jnp.dot(mine, b_mine, precision=HIGH) + jnp.dot(theirs, b_theirs, precision=HIGH)

    def piece(values):
        return lax.dynamic_slice(values, (xl * half, panel * blk), (half, blk)) * fill[row, column]

    def sum_x(parts):
        return jnp.sum(lax.all_to_all(parts, X, split_axis=0, concat_axis=0, tiled=True), axis=0)

    def finish(partial):
        return sum_x(partial.reshape(4, half, blk)) * keep[row, column]

    y_copies = jnp.broadcast_to(piece(y_blocks)[None], (ny, half, blk))
    z_piece = piece(z_blocks)
    y_copies, z_piece, z_blocks = lax.optimization_barrier((y_copies, z_piece, z_blocks))
    y_panel = lax.all_to_all(y_copies, "y", split_axis=0, concat_axis=0, tiled=True)
    y_panel = y_panel.reshape(ny * half, blk)
    t_own, t_other = [
        multiply(*rows, y_panel) for rows in rows_with_partner(*slices(z_blocks, fill))
    ]
    same = core == xh
    mine = jnp.where(same, t_own, t_other)
    theirs = swap(jnp.where(same, t_other, t_own), "core")
    even = (panel % 2) == 0
    blocks = jnp.stack([jnp.where(even, mine, theirs), jnp.where(even, theirs, mine)])
    blocks = blocks.reshape(2, blk, 2, half).transpose(0, 2, 1, 3).reshape(4, blk, half)
    t_share = sum_x(blocks)
    t_row = 2 * y + core
    source = (z ^ xh) & 1
    t_col = per_core * source + (z ^ source)
    at_row = t_row * blk + lax.broadcasted_iota(jnp.int32, (blk, half), 0)
    at_col = t_col * blk + xl * half + lax.broadcasted_iota(jnp.int32, (blk, half), 1)
    q_share = jnp.where(at_row == at_col, 1.5, 0.0) - 0.5 * (keep[t_row, t_col] * t_share)
    z_panel = lax.all_gather(z_piece, "y", axis=0)
    q_share, h_blocks = lax.optimization_barrier((q_share, h_blocks))
    q_mine = spread(q_share, "z", nz)
    h_part, h_rows = slices(h_blocks, h_pattern.astype(jnp.float32))
    q_mine, z_panel, h_part, h_rows = lax.optimization_barrier((q_mine, z_panel, h_part, h_rows))
    q_theirs = swap(q_mine, "core")
    ordered = z_panel.reshape(2, ny // 2, half, blk).transpose(1, 0, 2, 3)
    ordered = jnp.where(xh == 0, ordered, ordered[:, ::-1]).reshape(ny * half, blk)

    def rows_of(q):
        q = q.transpose(1, 0, 2).reshape(blk, nz * half)
        return jnp.dot(q, ordered, precision=HIGH)

    z_mine, z_theirs = rows_of(q_mine), rows_of(q_theirs)
    first = core == 0
    z_share = finish(
        jnp.stack([jnp.where(first, z_mine, z_theirs), jnp.where(first, z_theirs, z_mine)])
    )
    z_copies = jnp.broadcast_to(z_share[None], (ny, half, blk))
    z_copies, h_part, h_rows = lax.optimization_barrier((z_copies, h_part, h_rows))
    z_next_panel = lax.all_to_all(z_copies, "y", split_axis=0, concat_axis=0, tiled=True)
    z_next_panel = z_next_panel.reshape(ny * half, blk)
    z_shares = jnp.concatenate([z_share, swap(z_share, "xl")], axis=0)
    z_all = lax.all_gather(z_shares, "z", axis=0)
    h_own, h_other = [multiply(*rows, z_next_panel) for rows in rows_with_partner(h_part, h_rows)]
    h_partial = jnp.stack([jnp.where(xh == 0, h_own, h_other), jnp.where(xh == 0, h_other, h_own)])
    h_share = finish(h_partial)
    passed = half * 5 // 8
    rest = half - passed
    early = jnp.broadcast_to(h_share[:passed][None], (nz, passed, blk))
    early, h_share = lax.optimization_barrier((early, h_share))
    h_early = lax.all_to_all(early, "z", split_axis=0, concat_axis=0, tiled=True)
    late = jnp.concatenate([h_share[passed:], swap(h_share[passed:], "xl")], axis=0)
    late = jnp.broadcast_to(late[None], (nz, 2 * rest, blk))
    late, z_all, h_early = lax.optimization_barrier((late, z_all, h_early))
    h_late = lax.all_to_all(late, "z", split_axis=0, concat_axis=0, tiled=True)
    z_next = place([z_all], [(0, 0, 0, 0, half), (0, half, 1, 0, half)], blk)
    h_times_z = place(
        [h_early, h_late, swap(h_early, "xl")],
        [
            (0, 0, 0, 0, passed),
            (1, 0, 0, passed, rest),
            (1, rest, 1, passed, rest),
            (2, 0, 1, 0, passed),
        ],
        blk,
    )
    return (z_next, h_times_z)


def solution(mesh):
    parts = Mesh(mesh.devices.reshape(8, 2, 2, 8, 2), ("y", "xh", "core", "z", "xl"))
    spec = P(ROW, "core")
    return jax.shard_map(
        local,
        mesh=parts,
        in_specs=(spec, spec, spec, P(), P(), P()),
        out_specs=(spec, spec),
        check_vma=False,
    )
```

```python
import jax
import jax.numpy as jnp
from jax import lax
from jax.experimental import pallas as pl
from jax.experimental.pallas import tpu as pltpu
from jax.sharding import Mesh
from jax.sharding import PartitionSpec as P

X = ("xh", "xl")
ROW = ("y", "xh")
HIGH = lax.Precision.HIGH


def spread(piece, axis, n):
    copies = jnp.broadcast_to(piece[None], (n,) + piece.shape)
    return lax.all_to_all(copies, axis, split_axis=0, concat_axis=0, tiled=True)


def swap(array, axis):
    return lax.ppermute(array, axis, [(0, 1), (1, 0)])


def place(parts, pieces, blk):
    layers = parts[0].shape[0]
    half = blk // 2

    def kernel(*refs):
        out = refs[-1]
        xl = lax.axis_index("xl")
        core = lax.axis_index("core")
        for part, first, share, offset, rows in pieces:
            at = pl.multiple_of((xl ^ share) * half + offset, 8)
            for layer in range(layers):
                to = pl.multiple_of((layer ^ core) * blk, blk)
                out[pl.ds(at, rows), pl.ds(to, blk)] = refs[part][layer, first : first + rows]

    return pl.pallas_call(
        kernel,
        out_shape=jax.ShapeDtypeStruct((blk, layers * blk), parts[0].dtype),
        in_specs=[pl.BlockSpec(memory_space=pltpu.VMEM)] * len(parts),
        out_specs=pl.BlockSpec(memory_space=pltpu.VMEM),
        compiler_params=pltpu.CompilerParams(vmem_limit_bytes=24 * 1024 * 1024),
    )(*parts)


def local(y_blocks, z_blocks, h_blocks, s_pattern, h_pattern, keep_mask):
    blk, width = y_blocks.shape
    half = blk // 2
    per_core = width // blk
    ny, nz = lax.axis_size("y"), lax.axis_size("z")
    y = lax.axis_index("y")
    xh = lax.axis_index("xh")
    core = lax.axis_index("core")
    z = lax.axis_index("z")
    xl = lax.axis_index("xl")
    row = 2 * y + xh
    panel = z ^ core
    column = per_core * core + panel
    keep = keep_mask.astype(jnp.float32)
    fill = s_pattern.astype(jnp.float32)

    def slices(values, pattern, a, b):
        return jnp.concatenate(
            [
                lax.dynamic_slice(values, (0, (2 * m + a) * blk + b * half), (blk, half))
                * pattern[row, per_core * core + 2 * m + a]
                for m in range(per_core // 2)
            ],
            axis=1,
        )

    def from_partner(part):
        return lax.ppermute(part, X, [(0, 3), (3, 0), (1, 2), (2, 1)])

    def multiply(mine, theirs, b):
        inner = mine.shape[1]
        b_mine = lax.dynamic_slice_in_dim(b, core * inner, inner, 0)
        b_theirs = lax.dynamic_slice_in_dim(b, (1 - core) * inner, inner, 0)
        return jnp.dot(mine, b_mine, precision=HIGH) + jnp.dot(theirs, b_theirs, precision=HIGH)

    def piece(values):
        return lax.dynamic_slice(values, (xl * half, panel * blk), (half, blk)) * fill[row, column]

    def sum_x(parts):
        return jnp.sum(lax.all_to_all(parts, X, split_axis=0, concat_axis=0, tiled=True), axis=0)

    def finish(partial):
        return sum_x(partial.reshape(4, half, blk)) * keep[row, column]

    y_copies = jnp.broadcast_to(piece(y_blocks)[None], (ny, half, blk))
    z_piece = piece(z_blocks)
    y_copies, z_piece, z_blocks = lax.optimization_barrier((y_copies, z_piece, z_blocks))
    y_panel = lax.all_to_all(y_copies, "y", split_axis=0, concat_axis=0, tiled=True)
    y_panel = y_panel.reshape(ny * half, blk)
    z_part = slices(z_blocks, fill, 1 - xh, 1 - xl)
    z_part, z_blocks = lax.optimization_barrier((z_part, z_blocks))
    z_rows = slices(z_blocks, fill, xh, xl)
    t_own, t_other = [
        multiply(rows, swap(rows, "core"), y_panel) for rows in (z_rows, from_partner(z_part))
    ]
    same = core == xh
    mine = jnp.where(same, t_own, t_other)
    theirs = swap(jnp.where(same, t_other, t_own), "core")
    even = (panel % 2) == 0
    blocks = jnp.stack([jnp.where(even, mine, theirs), jnp.where(even, theirs, mine)])
    blocks = blocks.reshape(2, blk, 2, half).transpose(0, 2, 1, 3).reshape(4, blk, half)
    t_share = sum_x(blocks)
    t_row = 2 * y + core
    source = (z ^ xh) & 1
    t_col = per_core * source + (z ^ source)
    at_row = t_row * blk + lax.broadcasted_iota(jnp.int32, (blk, half), 0)
    at_col = t_col * blk + xl * half + lax.broadcasted_iota(jnp.int32, (blk, half), 1)
    q_share = jnp.where(at_row == at_col, 1.5, 0.0) - 0.5 * (keep[t_row, t_col] * t_share)
    z_panel = lax.all_gather(z_piece, "y", axis=0)
    q_share, h_blocks = lax.optimization_barrier((q_share, h_blocks))
    q_mine = spread(q_share, "z", nz)
    h_fill = h_pattern.astype(jnp.float32)
    h_others = from_partner(slices(h_blocks, h_fill, 1 - xh, 1 - xl))
    q_mine, z_panel, h_others = lax.optimization_barrier((q_mine, z_panel, h_others))
    q_theirs = swap(q_mine, "core")
    ordered = z_panel.reshape(2, ny // 2, half, blk).transpose(1, 0, 2, 3)
    ordered = jnp.where(xh == 0, ordered, ordered[:, ::-1]).reshape(ny * half, blk)

    def rows_of(q):
        q = q.transpose(1, 0, 2).reshape(blk, nz * half)
        return jnp.dot(q, ordered, precision=HIGH)

    z_mine, z_theirs = rows_of(q_mine), rows_of(q_theirs)
    first = core == 0
    z_share = finish(
        jnp.stack([jnp.where(first, z_mine, z_theirs), jnp.where(first, z_theirs, z_mine)])
    )
    z_copies = jnp.broadcast_to(z_share[None], (ny, half, blk))
    z_copies, h_others, h_blocks = lax.optimization_barrier((z_copies, h_others, h_blocks))
    h_rows = slices(h_blocks, h_fill, xh, xl)
    z_next_panel = lax.all_to_all(z_copies, "y", split_axis=0, concat_axis=0, tiled=True)
    z_next_panel = z_next_panel.reshape(ny * half, blk)
    z_shares = jnp.concatenate([z_share, swap(z_share, "xl")], axis=0)
    z_all = lax.all_gather(z_shares, "z", axis=0)
    h_own, h_other = [
        multiply(rows, swap(rows, "core"), z_next_panel) for rows in (h_rows, h_others)
    ]
    h_partial = jnp.stack([jnp.where(xh == 0, h_own, h_other), jnp.where(xh == 0, h_other, h_own)])
    h_share = finish(h_partial)
    passed = half * 5 // 8
    rest = half - passed
    early = jnp.broadcast_to(h_share[:passed][None], (nz, passed, blk))
    early, h_share = lax.optimization_barrier((early, h_share))
    h_early = lax.all_to_all(early, "z", split_axis=0, concat_axis=0, tiled=True)
    late = jnp.concatenate([h_share[passed:], swap(h_share[passed:], "xl")], axis=0)
    late = jnp.broadcast_to(late[None], (nz, 2 * rest, blk))
    late, z_all, h_early = lax.optimization_barrier((late, z_all, h_early))
    h_late = lax.all_to_all(late, "z", split_axis=0, concat_axis=0, tiled=True)
    z_next = place([z_all], [(0, 0, 0, 0, half), (0, half, 1, 0, half)], blk)
    h_times_z = place(
        [h_early, h_late, swap(h_early, "xl")],
        [
            (0, 0, 0, 0, passed),
            (1, 0, 0, passed, rest),
            (1, rest, 1, passed, rest),
            (2, 0, 1, 0, passed),
        ],
        blk,
    )
    return (z_next, h_times_z)


def solution(mesh):
    parts = Mesh(mesh.devices.reshape(8, 2, 2, 8, 2), ("y", "xh", "core", "z", "xl"))
    spec = P(ROW, "core")
    return jax.shard_map(
        local,
        mesh=parts,
        in_specs=(spec, spec, spec, P(), P(), P()),
        out_specs=(spec, spec),
        check_vma=False,
    )
```

```python
import jax
import jax.numpy as jnp
from jax import lax
from jax.experimental import pallas as pl
from jax.experimental.pallas import tpu as pltpu
from jax.sharding import Mesh
from jax.sharding import PartitionSpec as P

X = ("xh", "xl")
ROW = ("y", "xh")
HIGH = lax.Precision.HIGH


def spread(piece, axis, n):
    copies = jnp.broadcast_to(piece[None], (n,) + piece.shape)
    return lax.all_to_all(copies, axis, split_axis=0, concat_axis=0, tiled=True)


def swap(array, axis):
    return lax.ppermute(array, axis, [(0, 1), (1, 0)])


def place(parts, pieces, blk):
    layers = parts[0].shape[0]
    half = blk // 2

    def kernel(*refs):
        out = refs[-1]
        xl = lax.axis_index("xl")
        core = lax.axis_index("core")
        for part, first, share, offset, rows in pieces:
            at = pl.multiple_of((xl ^ share) * half + offset, 8)
            for layer in range(layers):
                to = pl.multiple_of((layer ^ core) * blk, blk)
                out[pl.ds(at, rows), pl.ds(to, blk)] = refs[part][layer, first : first + rows]

    return pl.pallas_call(
        kernel,
        out_shape=jax.ShapeDtypeStruct((blk, layers * blk), parts[0].dtype),
        in_specs=[pl.BlockSpec(memory_space=pltpu.VMEM)] * len(parts),
        out_specs=pl.BlockSpec(memory_space=pltpu.VMEM),
        compiler_params=pltpu.CompilerParams(vmem_limit_bytes=24 * 1024 * 1024),
    )(*parts)


def local(y_blocks, z_blocks, h_blocks, s_pattern, h_pattern, keep_mask):
    blk, width = y_blocks.shape
    half = blk // 2
    per_core = width // blk
    ny, nz = lax.axis_size("y"), lax.axis_size("z")
    y = lax.axis_index("y")
    xh = lax.axis_index("xh")
    core = lax.axis_index("core")
    z = lax.axis_index("z")
    xl = lax.axis_index("xl")
    row = 2 * y + xh
    panel = z ^ core
    column = per_core * core + panel
    keep = keep_mask.astype(jnp.float32)
    fill = s_pattern.astype(jnp.float32)

    def slices(values, pattern, a, b):
        return jnp.concatenate(
            [
                lax.dynamic_slice(values, (0, (2 * m + a) * blk + b * half), (blk, half))
                * pattern[row, per_core * core + 2 * m + a]
                for m in range(per_core // 2)
            ],
            axis=1,
        )

    def from_partner(part):
        return lax.ppermute(part, X, [(0, 3), (3, 0), (1, 2), (2, 1)])

    def multiply(mine, theirs, b):
        inner = mine.shape[1]
        b_mine = lax.dynamic_slice_in_dim(b, core * inner, inner, 0)
        b_theirs = lax.dynamic_slice_in_dim(b, (1 - core) * inner, inner, 0)
        return jnp.dot(mine, b_mine, precision=HIGH) + jnp.dot(theirs, b_theirs, precision=HIGH)

    def piece(values):
        return lax.dynamic_slice(values, (xl * half, panel * blk), (half, blk)) * fill[row, column]

    def sum_x(parts):
        return jnp.sum(lax.all_to_all(parts, X, split_axis=0, concat_axis=0, tiled=True), axis=0)

    def finish(partial):
        return sum_x(partial.reshape(4, half, blk)) * keep[row, column]

    y_copies = jnp.broadcast_to(piece(y_blocks)[None], (ny, half, blk))
    z_piece = piece(z_blocks)
    y_copies, z_piece, z_blocks = lax.optimization_barrier((y_copies, z_piece, z_blocks))
    y_panel = lax.all_to_all(y_copies, "y", split_axis=0, concat_axis=0, tiled=True)
    y_panel = y_panel.reshape(ny * half, blk)
    z_part = slices(z_blocks, fill, 1 - xh, 1 - xl)
    z_part, z_blocks = lax.optimization_barrier((z_part, z_blocks))
    z_rows = slices(z_blocks, fill, xh, xl)
    t_own, t_other = [
        multiply(rows, swap(rows, "core"), y_panel) for rows in (z_rows, from_partner(z_part))
    ]
    same = core == xh
    mine = jnp.where(same, t_own, t_other)
    theirs = swap(jnp.where(same, t_other, t_own), "core")
    even = (panel % 2) == 0
    blocks = jnp.stack([jnp.where(even, mine, theirs), jnp.where(even, theirs, mine)])
    blocks = blocks.reshape(2, blk, 2, half).transpose(0, 2, 1, 3).reshape(4, blk, half)
    t_share = sum_x(blocks)
    t_row = 2 * y + core
    source = (z ^ xh) & 1
    t_col = per_core * source + (z ^ source)
    at_row = t_row * blk + lax.broadcasted_iota(jnp.int32, (blk, half), 0)
    at_col = t_col * blk + xl * half + lax.broadcasted_iota(jnp.int32, (blk, half), 1)
    q_share = jnp.where(at_row == at_col, 1.5, 0.0) - 0.5 * (keep[t_row, t_col] * t_share)
    z_panel = lax.all_gather(z_piece, "y", axis=0)
    q_share, h_blocks = lax.optimization_barrier((q_share, h_blocks))
    q_mine = spread(q_share, "z", nz)
    h_fill = h_pattern.astype(jnp.float32)
    h_others = from_partner(slices(h_blocks, h_fill, 1 - xh, 1 - xl))
    q_mine, z_panel, h_others = lax.optimization_barrier((q_mine, z_panel, h_others))
    q_theirs = swap(q_mine, "core")
    ordered = z_panel.reshape(2, ny // 2, half, blk).transpose(1, 0, 2, 3)
    ordered = jnp.where(xh == 0, ordered, ordered[:, ::-1]).reshape(ny * half, blk)

    def rows_of(q):
        q = q.transpose(1, 0, 2).reshape(blk, nz * half)
        return jnp.dot(q, ordered, precision=HIGH)

    z_mine, z_theirs = rows_of(q_mine), rows_of(q_theirs)
    first = core == 0
    z_share = finish(
        jnp.stack([jnp.where(first, z_mine, z_theirs), jnp.where(first, z_theirs, z_mine)])
    )
    z_copies = jnp.broadcast_to(z_share[None], (ny, half, blk))
    z_copies, h_others, h_blocks = lax.optimization_barrier((z_copies, h_others, h_blocks))
    h_rows = slices(h_blocks, h_fill, xh, xl)
    z_next_panel = lax.all_to_all(z_copies, "y", split_axis=0, concat_axis=0, tiled=True)
    z_next_panel = z_next_panel.reshape(ny * half, blk)
    z_shares = jnp.concatenate([z_share, swap(z_share, "xl")], axis=0)
    z_all = lax.all_gather(z_shares, "z", axis=0)
    h_own, h_other = [
        multiply(rows, swap(rows, "core"), z_next_panel) for rows in (h_rows, h_others)
    ]
    h_partial = jnp.stack([jnp.where(xh == 0, h_own, h_other), jnp.where(xh == 0, h_other, h_own)])
    h_share = finish(h_partial)
    passed = half * 9 // 16
    rest = half - passed
    early = jnp.broadcast_to(h_share[:passed][None], (nz, passed, blk))
    early, h_share = lax.optimization_barrier((early, h_share))
    h_early = lax.all_to_all(early, "z", split_axis=0, concat_axis=0, tiled=True)
    late = jnp.concatenate([h_share[passed:], swap(h_share[passed:], "xl")], axis=0)
    z_next = place([z_all], [(0, 0, 0, 0, half), (0, half, 1, 0, half)], blk)
    h_early, z_next = lax.optimization_barrier((h_early, z_next))
    late, h_early = lax.optimization_barrier((late, h_early))
    h_late = lax.all_gather(late, "z", axis=0)
    h_times_z = place(
        [h_early, h_late, swap(h_early, "xl")],
        [
            (0, 0, 0, 0, passed),
            (1, 0, 0, passed, rest),
            (1, rest, 1, passed, rest),
            (2, 0, 1, 0, passed),
        ],
        blk,
    )
    return (z_next, h_times_z)


def solution(mesh):
    parts = Mesh(mesh.devices.reshape(8, 2, 2, 8, 2), ("y", "xh", "core", "z", "xl"))
    spec = P(ROW, "core")
    return jax.shard_map(
        local,
        mesh=parts,
        in_specs=(spec, spec, spec, P(), P(), P()),
        out_specs=(spec, spec),
        check_vma=False,
    )
```

```python
import jax
import jax.numpy as jnp
from jax import lax
from jax.experimental import pallas as pl
from jax.experimental.pallas import tpu as pltpu
from jax.sharding import Mesh
from jax.sharding import PartitionSpec as P

X = ("xh", "xl")
ROW = ("y", "xh")
HIGH = lax.Precision.HIGH


def spread(piece, axis, n):
    copies = jnp.broadcast_to(piece[None], (n,) + piece.shape)
    return lax.all_to_all(copies, axis, split_axis=0, concat_axis=0, tiled=True)


def swap(array, axis):
    return lax.ppermute(array, axis, [(0, 1), (1, 0)])


def place(parts, pieces, blk):
    layers = parts[0].shape[0]
    half = blk // 2

    def kernel(*refs):
        out = refs[-1]
        xl = lax.axis_index("xl")
        core = lax.axis_index("core")
        for part, first, share, offset, rows in pieces:
            at = pl.multiple_of((xl ^ share) * half + offset, 8)
            for layer in range(layers):
                to = pl.multiple_of((layer ^ core) * blk, blk)
                out[pl.ds(at, rows), pl.ds(to, blk)] = refs[part][layer, first : first + rows]

    return pl.pallas_call(
        kernel,
        out_shape=jax.ShapeDtypeStruct((blk, layers * blk), parts[0].dtype),
        in_specs=[pl.BlockSpec(memory_space=pltpu.VMEM)] * len(parts),
        out_specs=pl.BlockSpec(memory_space=pltpu.VMEM),
        compiler_params=pltpu.CompilerParams(vmem_limit_bytes=24 * 1024 * 1024),
    )(*parts)


def local(y_blocks, z_blocks, h_blocks, s_pattern, h_pattern, keep_mask):
    blk, width = y_blocks.shape
    half = blk // 2
    per_core = width // blk
    ny, nz = lax.axis_size("y"), lax.axis_size("z")
    y = lax.axis_index("y")
    xh = lax.axis_index("xh")
    core = lax.axis_index("core")
    z = lax.axis_index("z")
    xl = lax.axis_index("xl")
    row = 2 * y + xh
    panel = z ^ core
    column = per_core * core + panel
    keep = keep_mask.astype(jnp.float32)
    fill = s_pattern.astype(jnp.float32)

    def slices(values, pattern, a, b):
        return jnp.concatenate(
            [
                lax.dynamic_slice(values, (0, (2 * m + a) * blk + b * half), (blk, half))
                * pattern[row, per_core * core + 2 * m + a]
                for m in range(per_core // 2)
            ],
            axis=1,
        )

    def from_partner(part):
        return lax.ppermute(part, X, [(0, 3), (3, 0), (1, 2), (2, 1)])

    def multiply(mine, theirs, b):
        inner = mine.shape[1]
        b_mine = lax.dynamic_slice_in_dim(b, core * inner, inner, 0)
        b_theirs = lax.dynamic_slice_in_dim(b, (1 - core) * inner, inner, 0)
        return jnp.dot(mine, b_mine, precision=HIGH) + jnp.dot(theirs, b_theirs, precision=HIGH)

    def piece(values):
        return lax.dynamic_slice(values, (xl * half, panel * blk), (half, blk)) * fill[row, column]

    def sum_x(parts):
        return jnp.sum(lax.all_to_all(parts, X, split_axis=0, concat_axis=0, tiled=True), axis=0)

    def finish(partial):
        return sum_x(partial.reshape(4, half, blk)) * keep[row, column]

    y_copies = jnp.broadcast_to(piece(y_blocks)[None], (ny, half, blk))
    z_piece = piece(z_blocks)
    y_copies, z_piece, z_blocks = lax.optimization_barrier((y_copies, z_piece, z_blocks))
    y_panel = lax.all_to_all(y_copies, "y", split_axis=0, concat_axis=0, tiled=True)
    y_panel = y_panel.reshape(ny * half, blk)
    z_part = slices(z_blocks, fill, 1 - xh, 1 - xl)
    z_part, z_blocks = lax.optimization_barrier((z_part, z_blocks))
    z_rows = slices(z_blocks, fill, xh, xl)
    t_own, t_other = [
        multiply(rows, swap(rows, "core"), y_panel) for rows in (z_rows, from_partner(z_part))
    ]
    same = core == xh
    mine = jnp.where(same, t_own, t_other)
    theirs = swap(jnp.where(same, t_other, t_own), "core")
    even = (panel % 2) == 0
    blocks = jnp.stack([jnp.where(even, mine, theirs), jnp.where(even, theirs, mine)])
    blocks = blocks.reshape(2, blk, 2, half).transpose(0, 2, 1, 3).reshape(4, blk, half)
    t_share = sum_x(blocks)
    t_row = 2 * y + core
    source = (z ^ xh) & 1
    t_col = per_core * source + (z ^ source)
    at_row = t_row * blk + lax.broadcasted_iota(jnp.int32, (blk, half), 0)
    at_col = t_col * blk + xl * half + lax.broadcasted_iota(jnp.int32, (blk, half), 1)
    q_share = jnp.where(at_row == at_col, 1.5, 0.0) - 0.5 * (keep[t_row, t_col] * t_share)
    z_panel = lax.all_gather(z_piece, "y", axis=0)
    q_share, h_blocks = lax.optimization_barrier((q_share, h_blocks))
    q_mine = spread(q_share, "z", nz)
    h_fill = h_pattern.astype(jnp.float32)
    h_others = from_partner(slices(h_blocks, h_fill, 1 - xh, 1 - xl))
    q_mine, z_panel, h_others = lax.optimization_barrier((q_mine, z_panel, h_others))
    q_theirs = swap(q_mine, "core")
    ordered = z_panel.reshape(2, ny // 2, half, blk).transpose(1, 0, 2, 3)
    ordered = jnp.where(xh == 0, ordered, ordered[:, ::-1]).reshape(ny * half, blk)

    def rows_of(q):
        q = q.transpose(1, 0, 2).reshape(blk, nz * half)
        return jnp.dot(q, ordered, precision=HIGH)

    z_mine, z_theirs = rows_of(q_mine), rows_of(q_theirs)
    first = core == 0
    z_share = finish(
        jnp.stack([jnp.where(first, z_mine, z_theirs), jnp.where(first, z_theirs, z_mine)])
    )
    z_copies = jnp.broadcast_to(z_share[None], (ny, half, blk))
    z_copies, h_others, h_blocks = lax.optimization_barrier((z_copies, h_others, h_blocks))
    h_rows = slices(h_blocks, h_fill, xh, xl)
    z_next_panel = lax.all_to_all(z_copies, "y", split_axis=0, concat_axis=0, tiled=True)
    z_next_panel = z_next_panel.reshape(ny * half, blk)
    z_shares = jnp.concatenate([z_share, swap(z_share, "xl")], axis=0)
    z_all = lax.all_gather(z_shares, "z", axis=0)
    h_own, h_other = [
        multiply(rows, swap(rows, "core"), z_next_panel) for rows in (h_rows, h_others)
    ]
    h_partial = jnp.stack([jnp.where(xh == 0, h_own, h_other), jnp.where(xh == 0, h_other, h_own)])
    h_share = finish(h_partial)
    passed = half // 2
    rest = half - passed
    early = jnp.broadcast_to(h_share[:passed][None], (nz, passed, blk))
    h_early = lax.all_to_all(early, "z", split_axis=0, concat_axis=0, tiled=True)
    late = jnp.concatenate([h_share[passed:], swap(h_share[passed:], "xl")], axis=0)
    z_next = place([z_all], [(0, 0, 0, 0, half), (0, half, 1, 0, half)], blk)
    h_early, z_next = lax.optimization_barrier((h_early, z_next))
    h_late = lax.all_gather(late, "z", axis=0)
    h_times_z = place(
        [h_early, h_late, swap(h_early, "xl")],
        [
            (0, 0, 0, 0, passed),
            (1, 0, 0, passed, rest),
            (1, rest, 1, passed, rest),
            (2, 0, 1, 0, passed),
        ],
        blk,
    )
    return (z_next, h_times_z)


def solution(mesh):
    parts = Mesh(mesh.devices.reshape(8, 2, 2, 8, 2), ("y", "xh", "core", "z", "xl"))
    spec = P(ROW, "core")
    return jax.shard_map(
        local,
        mesh=parts,
        in_specs=(spec, spec, spec, P(), P(), P()),
        out_specs=(spec, spec),
        check_vma=False,
    )
```

```python
import jax
import jax.numpy as jnp
from jax import lax
from jax.experimental import pallas as pl
from jax.experimental.pallas import tpu as pltpu
from jax.sharding import Mesh
from jax.sharding import PartitionSpec as P

X = ("xh", "xl")
ROW = ("y", "xh")
HIGH = lax.Precision.HIGH


def spread(piece, axis, n):
    copies = jnp.broadcast_to(piece[None], (n,) + piece.shape)
    return lax.all_to_all(copies, axis, split_axis=0, concat_axis=0, tiled=True)


def swap(array, axis):
    return lax.ppermute(array, axis, [(0, 1), (1, 0)])


def place(parts, pieces, blk):
    layers = parts[0].shape[0]
    half = blk // 2

    def kernel(*refs):
        out = refs[-1]
        xl = lax.axis_index("xl")
        core = lax.axis_index("core")
        for part, first, share, offset, rows in pieces:
            at = pl.multiple_of((xl ^ share) * half + offset, 8)
            for layer in range(layers):
                to = pl.multiple_of((layer ^ core) * blk, blk)
                out[pl.ds(at, rows), pl.ds(to, blk)] = refs[part][layer, first : first + rows]

    return pl.pallas_call(
        kernel,
        out_shape=jax.ShapeDtypeStruct((blk, layers * blk), parts[0].dtype),
        in_specs=[pl.BlockSpec(memory_space=pltpu.VMEM)] * len(parts),
        out_specs=pl.BlockSpec(memory_space=pltpu.VMEM),
        compiler_params=pltpu.CompilerParams(vmem_limit_bytes=24 * 1024 * 1024),
    )(*parts)


def local(y_blocks, z_blocks, h_blocks, s_pattern, h_pattern, keep_mask):
    blk, width = y_blocks.shape
    half = blk // 2
    per_core = width // blk
    ny, nz = lax.axis_size("y"), lax.axis_size("z")
    y = lax.axis_index("y")
    xh = lax.axis_index("xh")
    core = lax.axis_index("core")
    z = lax.axis_index("z")
    xl = lax.axis_index("xl")
    row = 2 * y + xh
    panel = z ^ core
    column = per_core * core + panel
    keep = keep_mask.astype(jnp.float32)
    fill = s_pattern.astype(jnp.float32)

    def slices(values, pattern, a, b):
        return jnp.concatenate(
            [
                lax.dynamic_slice(values, (0, (2 * m + a) * blk + b * half), (blk, half))
                * pattern[row, per_core * core + 2 * m + a]
                for m in range(per_core // 2)
            ],
            axis=1,
        )

    def from_partner(part):
        return lax.ppermute(part, X, [(0, 3), (3, 0), (1, 2), (2, 1)])

    def multiply(mine, theirs, b):
        inner = mine.shape[1]
        b_mine = lax.dynamic_slice_in_dim(b, core * inner, inner, 0)
        b_theirs = lax.dynamic_slice_in_dim(b, (1 - core) * inner, inner, 0)
        return jnp.dot(mine, b_mine, precision=HIGH) + jnp.dot(theirs, b_theirs, precision=HIGH)

    def piece(values):
        return lax.dynamic_slice(values, (xl * half, panel * blk), (half, blk)) * fill[row, column]

    def sum_x(parts):
        return jnp.sum(lax.all_to_all(parts, X, split_axis=0, concat_axis=0, tiled=True), axis=0)

    def finish(partial):
        return sum_x(partial.reshape(4, half, blk)) * keep[row, column]

    y_copies = jnp.broadcast_to(piece(y_blocks)[None], (ny, half, blk))
    z_piece = piece(z_blocks)
    y_copies, z_piece, z_blocks = lax.optimization_barrier((y_copies, z_piece, z_blocks))
    y_panel = lax.all_to_all(y_copies, "y", split_axis=0, concat_axis=0, tiled=True)
    y_panel = y_panel.reshape(ny * half, blk)
    z_part = slices(z_blocks, fill, 1 - xh, 1 - xl)
    z_part, z_blocks = lax.optimization_barrier((z_part, z_blocks))
    z_rows = slices(z_blocks, fill, xh, xl)
    t_own, t_other = [
        multiply(rows, swap(rows, "core"), y_panel) for rows in (z_rows, from_partner(z_part))
    ]
    same = core == xh
    mine = jnp.where(same, t_own, t_other)
    theirs = swap(jnp.where(same, t_other, t_own), "core")
    even = (panel % 2) == 0
    blocks = jnp.stack([jnp.where(even, mine, theirs), jnp.where(even, theirs, mine)])
    blocks = blocks.reshape(2, blk, 2, half).transpose(0, 2, 1, 3).reshape(4, blk, half)
    t_share = sum_x(blocks)
    t_row = 2 * y + core
    source = (z ^ xh) & 1
    t_col = per_core * source + (z ^ source)
    at_row = t_row * blk + lax.broadcasted_iota(jnp.int32, (blk, half), 0)
    at_col = t_col * blk + xl * half + lax.broadcasted_iota(jnp.int32, (blk, half), 1)
    q_share = jnp.where(at_row == at_col, 1.5, 0.0) - 0.5 * (keep[t_row, t_col] * t_share)
    z_panel = lax.all_gather(z_piece, "y", axis=0)
    q_share, h_blocks = lax.optimization_barrier((q_share, h_blocks))
    q_mine = spread(q_share, "z", nz)
    h_fill = h_pattern.astype(jnp.float32)
    h_others = from_partner(slices(h_blocks, h_fill, 1 - xh, 1 - xl))
    q_mine, z_panel, h_others = lax.optimization_barrier((q_mine, z_panel, h_others))
    q_theirs = swap(q_mine, "core")
    ordered = z_panel.reshape(2, ny // 2, half, blk).transpose(1, 0, 2, 3)
    ordered = jnp.where(xh == 0, ordered, ordered[:, ::-1]).reshape(ny * half, blk)

    def rows_of(q):
        q = q.transpose(1, 0, 2).reshape(blk, nz * half)
        return jnp.dot(q, ordered, precision=HIGH)

    z_mine, z_theirs = rows_of(q_mine), rows_of(q_theirs)
    first = core == 0
    z_share = finish(
        jnp.stack([jnp.where(first, z_mine, z_theirs), jnp.where(first, z_theirs, z_mine)])
    )
    z_copies = jnp.broadcast_to(z_share[None], (ny, half, blk))
    z_copies, h_others, h_blocks = lax.optimization_barrier((z_copies, h_others, h_blocks))
    h_rows = slices(h_blocks, h_fill, xh, xl)
    z_next_panel = lax.all_to_all(z_copies, "y", split_axis=0, concat_axis=0, tiled=True)
    z_next_panel = z_next_panel.reshape(ny * half, blk)
    z_own = lax.all_gather(z_share, "z", axis=0)
    h_own, h_other = [
        multiply(rows, swap(rows, "core"), z_next_panel) for rows in (h_rows, h_others)
    ]
    h_partial = jnp.stack([jnp.where(xh == 0, h_own, h_other), jnp.where(xh == 0, h_other, h_own)])
    h_share = finish(h_partial)
    h_share, z_own = lax.optimization_barrier((h_share, z_own))
    passed = half * 3 // 8
    rest = half - passed
    early = jnp.broadcast_to(h_share[:passed][None], (nz, passed, blk))
    late = jnp.concatenate([h_share[passed:], swap(h_share[passed:], "xl")], axis=0)
    h_late = lax.all_gather(late, "z", axis=0)
    h_early = lax.all_to_all(early, "z", split_axis=0, concat_axis=0, tiled=True)
    z_other = swap(z_own, "xl")
    h_early, z_other = lax.optimization_barrier((h_early, z_other))
    z_next = place([z_own, z_other], [(0, 0, 0, 0, half), (1, 0, 1, 0, half)], blk)
    h_times_z = place(
        [h_early, h_late, swap(h_early, "xl")],
        [
            (0, 0, 0, 0, passed),
            (1, 0, 0, passed, rest),
            (1, rest, 1, passed, rest),
            (2, 0, 1, 0, passed),
        ],
        blk,
    )
    return (z_next, h_times_z)


def solution(mesh):
    parts = Mesh(mesh.devices.reshape(8, 2, 2, 8, 2), ("y", "xh", "core", "z", "xl"))
    spec = P(ROW, "core")
    return jax.shard_map(
        local,
        mesh=parts,
        in_specs=(spec, spec, spec, P(), P(), P()),
        out_specs=(spec, spec),
        check_vma=False,
    )
```

```python
import jax
import jax.numpy as jnp
from jax import lax
from jax.experimental import pallas as pl
from jax.experimental.pallas import tpu as pltpu
from jax.sharding import Mesh
from jax.sharding import PartitionSpec as P

X = ("xh", "xl")
ROW = ("y", "xh")
HIGH = lax.Precision.HIGH


def spread(piece, axis, n):
    copies = jnp.broadcast_to(piece[None], (n,) + piece.shape)
    return lax.all_to_all(copies, axis, split_axis=0, concat_axis=0, tiled=True)


def swap(array, axis):
    return lax.ppermute(array, axis, [(0, 1), (1, 0)])


def place(parts, pieces, blk):
    layers = parts[0].shape[0]
    half = blk // 2

    def kernel(*refs):
        out = refs[-1]
        xl = lax.axis_index("xl")
        core = lax.axis_index("core")
        for part, first, share, offset, rows in pieces:
            at = pl.multiple_of((xl ^ share) * half + offset, 8)
            for layer in range(layers):
                to = pl.multiple_of((layer ^ core) * blk, blk)
                out[pl.ds(at, rows), pl.ds(to, blk)] = refs[part][layer, first : first + rows]

    return pl.pallas_call(
        kernel,
        out_shape=jax.ShapeDtypeStruct((blk, layers * blk), parts[0].dtype),
        in_specs=[pl.BlockSpec(memory_space=pltpu.VMEM)] * len(parts),
        out_specs=pl.BlockSpec(memory_space=pltpu.VMEM),
        compiler_params=pltpu.CompilerParams(vmem_limit_bytes=24 * 1024 * 1024),
    )(*parts)


def local(y_blocks, z_blocks, h_blocks, s_pattern, h_pattern, keep_mask):
    blk, width = y_blocks.shape
    half = blk // 2
    per_core = width // blk
    ny, nz = lax.axis_size("y"), lax.axis_size("z")
    y = lax.axis_index("y")
    xh = lax.axis_index("xh")
    core = lax.axis_index("core")
    z = lax.axis_index("z")
    xl = lax.axis_index("xl")
    row = 2 * y + xh
    panel = z ^ core
    column = per_core * core + panel
    keep = keep_mask.astype(jnp.float32)
    fill = s_pattern.astype(jnp.float32)

    def slices(values, pattern, a, b):
        return jnp.concatenate(
            [
                lax.dynamic_slice(values, (0, (2 * m + a) * blk + b * half), (blk, half))
                * pattern[row, per_core * core + 2 * m + a]
                for m in range(per_core // 2)
            ],
            axis=1,
        )

    def from_partner(part):
        return lax.ppermute(part, X, [(0, 3), (3, 0), (1, 2), (2, 1)])

    def multiply(mine, theirs, b):
        inner = mine.shape[1]
        b_mine = lax.dynamic_slice_in_dim(b, core * inner, inner, 0)
        b_theirs = lax.dynamic_slice_in_dim(b, (1 - core) * inner, inner, 0)
        return jnp.dot(mine, b_mine, precision=HIGH) + jnp.dot(theirs, b_theirs, precision=HIGH)

    def piece(values):
        return lax.dynamic_slice(values, (xl * half, panel * blk), (half, blk)) * fill[row, column]

    def sum_x(parts):
        return jnp.sum(lax.all_to_all(parts, X, split_axis=0, concat_axis=0, tiled=True), axis=0)

    def finish(partial):
        return sum_x(partial.reshape(4, half, blk)) * keep[row, column]

    y_copies = jnp.broadcast_to(piece(y_blocks)[None], (ny, half, blk))
    z_piece = piece(z_blocks)
    y_copies, z_piece, z_blocks = lax.optimization_barrier((y_copies, z_piece, z_blocks))
    y_panel = lax.all_to_all(y_copies, "y", split_axis=0, concat_axis=0, tiled=True)
    y_panel = y_panel.reshape(ny * half, blk)
    z_part = slices(z_blocks, fill, 1 - xh, 1 - xl)
    z_part, z_blocks = lax.optimization_barrier((z_part, z_blocks))
    z_rows = slices(z_blocks, fill, xh, xl)
    t_own, t_other = [
        multiply(rows, swap(rows, "core"), y_panel) for rows in (z_rows, from_partner(z_part))
    ]
    same = core == xh
    mine = jnp.where(same, t_own, t_other)
    theirs = swap(jnp.where(same, t_other, t_own), "core")
    even = (panel % 2) == 0
    blocks = jnp.stack([jnp.where(even, mine, theirs), jnp.where(even, theirs, mine)])
    blocks = blocks.reshape(2, blk, 2, half).transpose(0, 2, 1, 3).reshape(4, blk, half)
    t_share = sum_x(blocks)
    t_row = 2 * y + core
    source = (z ^ xh) & 1
    t_col = per_core * source + (z ^ source)
    at_row = t_row * blk + lax.broadcasted_iota(jnp.int32, (blk, half), 0)
    at_col = t_col * blk + xl * half + lax.broadcasted_iota(jnp.int32, (blk, half), 1)
    q_share = jnp.where(at_row == at_col, 1.5, 0.0) - 0.5 * (keep[t_row, t_col] * t_share)
    z_panel = lax.all_gather(z_piece, "y", axis=0)
    q_share, h_blocks = lax.optimization_barrier((q_share, h_blocks))
    q_mine = spread(q_share, "z", nz)
    h_fill = h_pattern.astype(jnp.float32)
    h_others = from_partner(slices(h_blocks, h_fill, 1 - xh, 1 - xl))
    q_mine, z_panel, h_others = lax.optimization_barrier((q_mine, z_panel, h_others))
    q_theirs = swap(q_mine, "core")
    ordered = z_panel.reshape(2, ny // 2, half, blk).transpose(1, 0, 2, 3)
    ordered = jnp.where(xh == 0, ordered, ordered[:, ::-1]).reshape(ny * half, blk)

    def rows_of(q):
        q = q.transpose(1, 0, 2).reshape(blk, nz * half)
        return jnp.dot(q, ordered, precision=HIGH)

    z_mine, z_theirs = rows_of(q_mine), rows_of(q_theirs)
    first = core == 0
    z_share = finish(
        jnp.stack([jnp.where(first, z_mine, z_theirs), jnp.where(first, z_theirs, z_mine)])
    )
    z_copies = jnp.broadcast_to(z_share[None], (ny, half, blk))
    z_copies, h_others, h_blocks = lax.optimization_barrier((z_copies, h_others, h_blocks))
    h_rows = slices(h_blocks, h_fill, xh, xl)
    z_next_panel = lax.all_to_all(z_copies, "y", split_axis=0, concat_axis=0, tiled=True)
    z_next_panel = z_next_panel.reshape(ny * half, blk)
    z_own = lax.all_gather(z_share, "z", axis=0)
    h_own, h_other = [
        multiply(rows, swap(rows, "core"), z_next_panel) for rows in (h_rows, h_others)
    ]
    h_partial = jnp.stack([jnp.where(xh == 0, h_own, h_other), jnp.where(xh == 0, h_other, h_own)])
    h_share = finish(h_partial)
    h_share, z_own = lax.optimization_barrier((h_share, z_own))
    passed = half // 2
    rest = half - passed
    early = jnp.broadcast_to(h_share[:passed][None], (nz, passed, blk))
    late = jnp.concatenate([h_share[passed:], swap(h_share[passed:], "xl")], axis=0)
    h_late = lax.all_gather(late, "z", axis=0)
    h_early = lax.all_to_all(early, "z", split_axis=0, concat_axis=0, tiled=True)
    z_other = swap(z_own, "xl")
    h_early, z_other = lax.optimization_barrier((h_early, z_other))
    z_next = place([z_own, z_other], [(0, 0, 0, 0, half), (1, 0, 1, 0, half)], blk)
    h_times_z = place(
        [h_early, h_late, swap(h_early, "xl")],
        [
            (0, 0, 0, 0, passed),
            (1, 0, 0, passed, rest),
            (1, rest, 1, passed, rest),
            (2, 0, 1, 0, passed),
        ],
        blk,
    )
    return (z_next, h_times_z)


def solution(mesh):
    parts = Mesh(mesh.devices.reshape(8, 2, 2, 8, 2), ("y", "xh", "core", "z", "xl"))
    spec = P(ROW, "core")
    return jax.shard_map(
        local,
        mesh=parts,
        in_specs=(spec, spec, spec, P(), P(), P()),
        out_specs=(spec, spec),
        check_vma=False,
    )
```

```python
import jax
import jax.numpy as jnp
from jax import lax
from jax.experimental import pallas as pl
from jax.experimental.pallas import tpu as pltpu
from jax.sharding import Mesh
from jax.sharding import PartitionSpec as P

X = ("xh", "xl")
ROW = ("y", "xh")
HIGH = lax.Precision.HIGH


def spread(piece, axis, n):
    copies = jnp.broadcast_to(piece[None], (n,) + piece.shape)
    return lax.all_to_all(copies, axis, split_axis=0, concat_axis=0, tiled=True)


def swap(array, axis):
    return lax.ppermute(array, axis, [(0, 1), (1, 0)])


def place(parts, pieces, blk):
    layers = parts[0].shape[0]
    half = blk // 2

    def kernel(*refs):
        out = refs[-1]
        xl = lax.axis_index("xl")
        core = lax.axis_index("core")
        for part, first, share, offset, rows in pieces:
            at = pl.multiple_of((xl ^ share) * half + offset, 8)
            for layer in range(layers):
                to = pl.multiple_of((layer ^ core) * blk, blk)
                out[pl.ds(at, rows), pl.ds(to, blk)] = refs[part][layer, first : first + rows]

    return pl.pallas_call(
        kernel,
        out_shape=jax.ShapeDtypeStruct((blk, layers * blk), parts[0].dtype),
        in_specs=[pl.BlockSpec(memory_space=pltpu.VMEM)] * len(parts),
        out_specs=pl.BlockSpec(memory_space=pltpu.VMEM),
        compiler_params=pltpu.CompilerParams(vmem_limit_bytes=24 * 1024 * 1024),
    )(*parts)


def local(y_blocks, z_blocks, h_blocks, s_pattern, h_pattern, keep_mask):
    blk, width = y_blocks.shape
    half = blk // 2
    per_core = width // blk
    ny, nz = lax.axis_size("y"), lax.axis_size("z")
    y = lax.axis_index("y")
    xh = lax.axis_index("xh")
    core = lax.axis_index("core")
    z = lax.axis_index("z")
    xl = lax.axis_index("xl")
    row = 2 * y + xh
    panel = z ^ core
    column = per_core * core + panel

    def entry(pattern, a, b):
        return lax.dynamic_slice(pattern, (a, b), (1, 1)).astype(jnp.float32)

    def slices(values, pattern, a, b):
        return jnp.concatenate(
            [
                lax.dynamic_slice(values, (0, (2 * m + a) * blk + b * half), (blk, half))
                * entry(pattern, row, per_core * core + 2 * m + a)
                for m in range(per_core // 2)
            ],
            axis=1,
        )

    def from_partner(part):
        return lax.ppermute(part, X, [(0, 3), (3, 0), (1, 2), (2, 1)])

    def multiply(mine, theirs, b):
        inner = mine.shape[1]
        b_mine = lax.dynamic_slice_in_dim(b, core * inner, inner, 0)
        b_theirs = lax.dynamic_slice_in_dim(b, (1 - core) * inner, inner, 0)
        return jnp.dot(mine, b_mine, precision=HIGH) + jnp.dot(theirs, b_theirs, precision=HIGH)

    def piece(values):
        return lax.dynamic_slice(values, (xl * half, panel * blk), (half, blk)) * entry(s_pattern, row, column)

    def sum_x(parts):
        return jnp.sum(lax.all_to_all(parts, X, split_axis=0, concat_axis=0, tiled=True), axis=0)

    def finish(partial):
        return sum_x(partial.reshape(4, half, blk)) * entry(keep_mask, row, column)

    y_copies = jnp.broadcast_to(piece(y_blocks)[None], (ny, half, blk))
    y_copies, z_blocks = lax.optimization_barrier((y_copies, z_blocks))
    y_panel = lax.all_to_all(y_copies, "y", split_axis=0, concat_axis=0, tiled=True)
    y_panel = y_panel.reshape(ny * half, blk)
    z_part, z_piece = slices(z_blocks, s_pattern, 1 - xh, 1 - xl), piece(z_blocks)
    z_part, z_piece, z_blocks = lax.optimization_barrier((z_part, z_piece, z_blocks))
    z_panel = lax.all_gather(z_piece, "y", axis=0)
    z_rows = slices(z_blocks, s_pattern, xh, xl)
    t_own, t_other = [
        multiply(rows, swap(rows, "core"), y_panel) for rows in (z_rows, from_partner(z_part))
    ]
    same = core == xh
    mine = jnp.where(same, t_own, t_other)
    theirs = swap(jnp.where(same, t_other, t_own), "core")
    even = (panel % 2) == 0
    blocks = jnp.stack([jnp.where(even, mine, theirs), jnp.where(even, theirs, mine)])
    blocks = blocks.reshape(2, blk, 2, half).transpose(0, 2, 1, 3).reshape(4, blk, half)
    t_share = sum_x(blocks)
    t_row = 2 * y + core
    source = (z ^ xh) & 1
    t_col = per_core * source + (z ^ source)
    at_row = t_row * blk + lax.broadcasted_iota(jnp.int32, (blk, half), 0)
    at_col = t_col * blk + xl * half + lax.broadcasted_iota(jnp.int32, (blk, half), 1)
    q_share = jnp.where(at_row == at_col, 1.5, 0.0) - 0.5 * (entry(keep_mask, t_row, t_col) * t_share)
    q_share, h_blocks = lax.optimization_barrier((q_share, h_blocks))
    q_mine = spread(q_share, "z", nz)
    h_others = from_partner(slices(h_blocks, h_pattern, 1 - xh, 1 - xl))
    q_mine, z_panel, h_others = lax.optimization_barrier((q_mine, z_panel, h_others))
    q_theirs = swap(q_mine, "core")
    ordered = z_panel.reshape(2, ny // 2, half, blk).transpose(1, 0, 2, 3)
    ordered = jnp.where(xh == 0, ordered, ordered[:, ::-1]).reshape(ny * half, blk)

    def rows_of(q):
        q = q.transpose(1, 0, 2).reshape(blk, nz * half)
        return jnp.dot(q, ordered, precision=HIGH)

    z_mine, z_theirs = rows_of(q_mine), rows_of(q_theirs)
    first = core == 0
    z_share = finish(
        jnp.stack([jnp.where(first, z_mine, z_theirs), jnp.where(first, z_theirs, z_mine)])
    )
    z_copies = jnp.broadcast_to(z_share[None], (ny, half, blk))
    z_copies, h_others, h_blocks = lax.optimization_barrier((z_copies, h_others, h_blocks))
    h_rows = slices(h_blocks, h_pattern, xh, xl)
    z_next_panel = lax.all_to_all(z_copies, "y", split_axis=0, concat_axis=0, tiled=True)
    z_next_panel = z_next_panel.reshape(ny * half, blk)
    z_shares = jnp.concatenate([z_share, swap(z_share, "xl")], axis=0)
    z_all = lax.all_gather(z_shares, "z", axis=0)
    h_own, h_other = [
        multiply(rows, swap(rows, "core"), z_next_panel) for rows in (h_rows, h_others)
    ]
    h_partial = jnp.stack([jnp.where(xh == 0, h_own, h_other), jnp.where(xh == 0, h_other, h_own)])
    h_share = finish(h_partial)
    passed = half // 2
    rest = half - passed
    early = jnp.broadcast_to(h_share[:passed][None], (nz, passed, blk))
    h_early = lax.all_to_all(early, "z", split_axis=0, concat_axis=0, tiled=True)
    late = jnp.concatenate([h_share[passed:], swap(h_share[passed:], "xl")], axis=0)
    z_next = place([z_all], [(0, 0, 0, 0, half), (0, half, 1, 0, half)], blk)
    h_early, z_next = lax.optimization_barrier((h_early, z_next))
    h_late = lax.all_gather(late, "z", axis=0)
    h_times_z = place(
        [h_early, h_late, swap(h_early, "xl")],
        [
            (0, 0, 0, 0, passed),
            (1, 0, 0, passed, rest),
            (1, rest, 1, passed, rest),
            (2, 0, 1, 0, passed),
        ],
        blk,
    )
    return (z_next, h_times_z)


def solution(mesh):
    parts = Mesh(mesh.devices.reshape(8, 2, 2, 8, 2), ("y", "xh", "core", "z", "xl"))
    spec = P(ROW, "core")
    return jax.shard_map(
        local,
        mesh=parts,
        in_specs=(spec, spec, spec, P(), P(), P()),
        out_specs=(spec, spec),
        check_vma=False,
    )
```
